512 devices in a mesh: dp: 128 (over x, z_hi, y), pair: 4 (over z_lo, core).
Axes of the slice: x: 4, y: 8, z: 8 (z_hi: 4, z_lo: 2; z = z_hi * 2 + z_lo), core: 2. Of those that a mesh axis runs over, the one named last changes fastest.
Arguments:
- student: bfloat16 [65536, 768], P(('dp', 'pair')), may hold values from -6 to 6
- teacher: bfloat16 [65536, 768], P(('dp', 'pair')), may hold values from -6 to 6
- band_codes: int32 [5], replicated, may hold values from 1 to 8
Outputs:
- block_loss: float32 [128, 4], P('dp', 'pair')
- student_grad: float32 [65536, 768], P(('dp', 'pair'))
The draws below stay inside these ranges and needn't reach their ends.
Inputs may be any that keep to these rules, and one draw needn't show every extreme that they name: Kernel m spreads over squared distances of about band_codes[m] * 384.
All inputs are finite; a program needn't handle non-finite values.
Results may differ from the reference program's by a relative error of at most 0.0019.
Values may be sent and summed in bfloat16 or wider, within the bound.
A program may use at most 64 MiB of HBM per device.

```python
import jax
import jax.numpy as jnp
from jax import lax

FEAT = 768
BANDS = 5
ROWS = 512
SAMPLES = 65536
N_DP = 128
N_PAIR = 4


def place_ends(drawn, stream_key, low, high):
    spot = [jax.random.randint(jax.random.fold_in(stream_key, axis), (), 0, length) for axis, length in enumerate(drawn.shape)]
    main_axis = drawn.shape.index(max(drawn.shape))
    neighbour = spot[:main_axis] + [(spot[main_axis] + 1) % drawn.shape[main_axis]] + spot[main_axis + 1:]
    return drawn.at[tuple(spot)].set(low).at[tuple(neighbour)].set(high)


def levels(stream_key, dims, split, smallest, largest):
    factor_of, own = 1.0, jax.random.fold_in(stream_key, 6)
    for position, shards_of in split:
        steps = jnp.exp(jax.random.uniform(jax.random.fold_in(own, position), (shards_of,), jnp.float32, smallest / len(split), largest / len(split)))
        factor_of = factor_of * jnp.repeat(steps, dims[position] // shards_of).reshape([-1 if axis == position else 1 for axis in range(len(dims))])
    return factor_of


def normal_values(key, extent, scale, bound, shards=(), kind=jnp.bfloat16):
    values = scale * jax.random.normal(key, extent, jnp.float32)
    if shards:
        values = values * levels(key, extent, shards, -0.22, 0.18)
    return jnp.clip(values, -bound, bound).astype(kind)


def setup_inputs(seed: int = 0) -> dict:
    key_of = jax.random.split(jax.random.key(seed), 4)
    student = normal_values(key_of[0], (SAMPLES, FEAT), 1.0, 6.0, ((0, 512),))
    teacher = normal_values(key_of[1], (SAMPLES, FEAT), 1.0, 6.0, ((0, 512),))
    band_codes = place_ends(jax.random.randint(key_of[2], (BANDS,), 1, 9), jax.random.fold_in(key_of[2], 1), 1, 8).astype(jnp.int32)
    return dict(student=student, teacher=teacher, band_codes=band_codes)


def squares(block):
    return jnp.sum(jnp.square(block.astype(jnp.float32)), axis=1)


def kernels(left_rows, right_rows, band_codes):
    width = left_rows.shape[1]
    inner = lax.dot_general(left_rows, right_rows, (((1,), (1,)), ((), ())), preferred_element_type=jnp.float32)
    dist = squares(left_rows)[:, None] + squares(right_rows)[None, :] - 2.0 * inner
    value = jnp.zeros_like(dist)
    slope = jnp.zeros_like(dist)
    for index in range(band_codes.shape[0]):
        scale = 2.0 / (band_codes[index].astype(jnp.float32) * width)
        term = jnp.exp(-scale * dist)
        value = value + term
        slope = slope + scale * term
    return value, slope


def transposed(coeff, rows):
    return lax.dot_general(coeff, rows, (((0,), (0,)), ((), ())), preferred_element_type=jnp.float32)


def pair_terms(own, other, band_codes):
    own_s, own_t = own[0], own[1]
    oth_s, oth_t = other[0], other[1]
    count = own.shape[1]
    width = own.shape[2]
    g_ss, h_ss = kernels(own_s, oth_s, band_codes)
    g_tt, h_tt = kernels(own_t, oth_t, band_codes)
    g_st, h_st = kernels(own_s, oth_t, band_codes)
    g_ts, h_ts = kernels(own_t, oth_s, band_codes)
    loss = jnp.sum(g_ss + g_tt - g_st - g_ts) / count
    factor = 2.0 * width / count
    c_ss = factor * h_ss
    c_st = factor * h_st
    c_ts = factor * h_ts
    e_ss = c_ss.astype(jnp.bfloat16)
    e_st = c_st.astype(jnp.bfloat16)
    e_ts = c_ts.astype(jnp.bfloat16)
    left = (jnp.sum(c_st, axis=1) - jnp.sum(c_ss, axis=1))[:, None] * own_s.astype(jnp.float32)
    left = left + jnp.dot(e_ss, oth_s, preferred_element_type=jnp.float32) - jnp.dot(e_st, oth_t, preferred_element_type=jnp.float32)
    right = (jnp.sum(c_ts, axis=0) - jnp.sum(c_ss, axis=0))[:, None] * oth_s.astype(jnp.float32)
    right = right + transposed(e_ss, own_s) - transposed(e_ts, own_t)
    return loss, left, right


def reference(student, teacher, band_codes):
    blocks = jnp.stack([student, teacher]).reshape(2, N_DP, ROWS, FEAT).transpose(1, 0, 2, 3)
    grad = jnp.zeros((N_DP, ROWS, FEAT), jnp.float32)
    losses = []
    for offset in range(N_PAIR):
        others = jnp.roll(blocks, -offset, axis=0)
        loss, left, right = lax.map(lambda duo: pair_terms(duo[0], duo[1], band_codes), (blocks, others))
        grad = grad + left + jnp.roll(right, offset, axis=0)
        losses.append(loss)
    block_loss = jnp.stack(losses, axis=1)
    return block_loss, grad.reshape(N_DP * ROWS, FEAT)
```

```python
import jax
import jax.numpy as jnp
from jax import lax
from jax.experimental import pallas as pl
from jax.experimental.pallas import tpu as pltpu
from jax.sharding import PartitionSpec as P

REACH = 3
LOG2E = 1.4426950408889634


def kernel(student, teacher, codes, loss_out, grad_out,
           bb, cbuf, nb, nc, inner, ebuf, acc, rows_acc, loss_acc, loss_in, got, z_out, z_in,
           local_sem, dp_send, dp_recv, pair_send, pair_recv, fin_send, fin_recv, loss_send, loss_recv):
    n_dp = lax.axis_size("dp")
    part, width = student.shape
    count = 4 * part
    bands = codes.shape[0]
    b = lax.axis_index("dp")
    p = lax.axis_index("pair")
    z_lo = p // 2
    core = p % 2
    sib = z_lo * 2 + (1 - core)
    zp = (1 - z_lo) * 2 + core
    diag = (1 - z_lo) * 2 + (1 - core)
    up = (b + 1) % n_dp
    down = (b + n_dp - 1) % n_dp

    def dev(block, place):
        return {"dp": block, "pair": place}

    def rows_of(q, chunk):
        return pl.ds(pl.multiple_of(chunk * count + q * part, part), part)

    barrier = pltpu.get_barrier_semaphore()
    for target in (dev(up, p), dev(down, p), dev(b, sib), dev(b, zp), dev(b, diag)):
        pl.semaphore_signal(barrier, inc=1, device_id=target, device_id_type=pl.DeviceIdType.MESH)
    pl.semaphore_wait(barrier, 5)

    own = (student, teacher)

    def remote(src, dst, ssem, rsem, target):
        return pltpu.make_async_remote_copy(
            src_ref=src, dst_ref=dst, send_sem=ssem, recv_sem=rsem,
            device_id=target, device_id_type=pl.DeviceIdType.MESH)

    def half(slot, chunk):
        return cbuf.at[slot, pl.ds(chunk * part, part)]

    def dp_copy(way, step, chunk):
        sign = -1 if way == 0 else 1
        src = own[chunk] if step == 1 else half(REACH + sign * (step - 1), chunk)
        dst = half(REACH + sign * step, chunk)
        return remote(src, dst, dp_send.at[way, step - 1, chunk], dp_recv.at[way, step - 1, chunk],
                      dev(up if way == 0 else down, p))

    def pair_copy(rel, chunk):
        if rel == 2:
            src = dst = bb.at[rows_of(zp, chunk)]
        else:
            src, dst = own[chunk], bb.at[rows_of(p, chunk)]
        target = dev(b, zp if rel == 1 else sib)
        return remote(src, dst, pair_send.at[rel, chunk], pair_recv.at[rel, chunk], target)

    def pair_arrived(rel, chunk):
        q = (sib, zp, diag)[rel]
        ref = bb.at[rows_of(q, chunk)]
        remote(ref, ref, pair_send.at[rel, chunk], pair_recv.at[rel, chunk], dev(b, sib)).wait_recv()

    local = [pltpu.make_async_copy(own[c], half(REACH, c), local_sem.at[0, c]) for c in (0, 1)]
    local += [pltpu.make_async_copy(own[c], bb.at[rows_of(p, c)], local_sem.at[1, c]) for c in (0, 1)]
    for chunk in (0, 1):
        for way in (0, 1):
            dp_copy(way, 1, chunk).start()
        pair_copy(1, chunk).start()
    for chunk in (0, 1):
        pair_copy(0, chunk).start()
    for c in local:
        c.start()

    scale = [2.0 / (codes[m].astype(jnp.float32) * width) for m in range(bands)]
    expo = [s * (-LOG2E) for s in scale]
    factor = 2.0 * width / count
    slope = [s * factor for s in scale]

    acc[...] = jnp.zeros_like(acc)
    rows_acc[...] = jnp.zeros_like(rows_acc)
    loss_acc[...] = jnp.zeros_like(loss_acc)

    def split_squares(x):
        sq = jnp.square(x.astype(jnp.float32))
        hi = sq.astype(jnp.bfloat16)
        lo = (sq - hi.astype(jnp.float32)).astype(jnp.bfloat16)
        return hi, lo

    def nt(x, y):
        return lax.dot_general(x, y, (((1,), (1,)), ((), ())), preferred_element_type=jnp.float32)

    def row_norms(q, chunk):
        here = rows_of(q, chunk)
        hi, lo = split_squares(bb[here, :])
        ones = jnp.ones((128, width), jnp.bfloat16)
        nb[here, :] = nt(hi, ones) + nt(lo, ones)

    def col_norms(slot):
        hi, lo = split_squares(cbuf[slot])
        ones = jnp.ones((8, width), jnp.bfloat16)
        nc[slot] = nt(ones, hi) + nt(ones, lo)

    step_rows = 32

    def work(offset):
        slot = REACH + offset
        ahead = offset >= 0
        weight = [2.0 * w for w in slope] if offset == 0 else slope
        col_norms(slot)
        cols = cbuf[slot]
        inner[pl.ds(0, count), :] = nt(bb[pl.ds(0, count), :], cols)
        if ahead:
            inner[pl.ds(count, count), :] = nt(bb[pl.ds(count, count), :], cols)

        def dist(here, at):
            norm = nb[here, :] + nc[slot, 0:1, pl.ds(at * part, part)]
            return norm - 2.0 * inner[here, pl.ds(at * part, part)]

        def sums(d, want_value, want_slope):
            value = slope_sum = None
            for m in range(bands):
                term = jnp.exp2(d * expo[m])
                if want_value:
                    value = term if value is None else value + term
                if want_slope:
                    scaled = term * weight[m]
                    slope_sum = scaled if slope_sum is None else slope_sum + scaled
            return value, slope_sum

        def fold(x):
            return jnp.sum(x.reshape(step_rows // 8, 8, part), axis=0)

        def body(i, total):
            here = pl.ds(pl.multiple_of(i * step_rows, step_rows), step_rows)
            g_ss, c_ss = sums(dist(here, 0), ahead, True)
            g_st, c_st = sums(dist(here, 1), ahead, True)
            ebuf[here, pl.ds(0, part)] = c_ss.astype(jnp.bfloat16)
            ebuf[here, pl.ds(part, part)] = (-c_st).astype(jnp.bfloat16)
            rows_acc[here, :] += c_st - c_ss
            if ahead:
                total = total + fold(g_ss - g_st)
                there = pl.ds(pl.multiple_of(count + i * step_rows, step_rows), step_rows)
                g_ts, _ = sums(dist(there, 0), True, False)
                g_tt, _ = sums(dist(there, 1), True, False)
                total = total + fold(g_tt - g_ts)
            return total

        total = lax.fori_loop(0, count // step_rows, body, jnp.zeros((8, part), jnp.float32))
        if ahead:
            loss_acc[offset] = total
        acc[...] += jnp.dot(ebuf[...], cols, preferred_element_type=jnp.float32)

    def arrived(step, chunk):
        for way in (0, 1):
            dp_copy(way, step, chunk).wait_recv()
            if step < REACH:
                dp_copy(way, step + 1, chunk).start()

    for c in local:
        c.wait()
    for chunk in (0, 1):
        row_norms(p, chunk)
        pair_arrived(0, chunk)
        row_norms(sib, chunk)
    for chunk in (0, 1):
        arrived(1, chunk)
        pair_arrived(1, chunk)
        pair_copy(2, chunk).start()
        row_norms(zp, chunk)
    for chunk in (0, 1):
        pair_arrived(2, chunk)
        row_norms(diag, chunk)
    work(0)
    work(1)
    arrived(2, 0)
    work(-1)
    arrived(2, 1)
    work(2)
    work(-2)
    arrived(3, 0)
    arrived(3, 1)
    work(3)
    work(-3)

    def loss_copy(rel):
        q = (sib, zp, diag)[rel]
        return remote(loss_acc.at[q], loss_in.at[rel], loss_send.at[rel], loss_recv.at[rel], dev(b, q))

    for rel in range(3):
        loss_copy(rel).start()

    def finish(q):
        here = pl.ds(pl.multiple_of(q * part, part), part)
        row = jnp.sum(rows_acc[here, :], axis=1, keepdims=True)
        acc[here, :] += row * bb[here, :].astype(jnp.float32)

    def sib_copy(which):
        q = (diag, sib)[which]
        here = pl.ds(pl.multiple_of(q * part, part), part)
        return remote(acc.at[here], got.at[which], fin_send.at[which], fin_recv.at[which], dev(b, sib))

    finish(diag)
    sib_copy(0).start()
    finish(sib)
    sib_copy(1).start()
    finish(zp)
    finish(p)
    sib_copy(0).wait_recv()
    zrow = pl.ds(pl.multiple_of(zp * part, part), part)
    z_out[...] = acc[zrow, :] + got[0]
    z_copy = remote(z_out, z_in, fin_send.at[2], fin_recv.at[2], dev(b, zp))
    z_copy.start()
    sib_copy(1).wait_recv()
    prow = pl.ds(pl.multiple_of(p * part, part), part)
    mine = acc[prow, :] + got[1]
    for rel in range(3):
        loss_copy(rel).wait_recv()
    total = loss_acc[p] + loss_in[0] + loss_in[1] + loss_in[2]
    loss_out[...] = jnp.sum(jnp.sum(total, axis=1, keepdims=True), axis=0, keepdims=True) * (1.0 / count)
    z_copy.wait_recv()
    grad_out[...] = mine + z_in[...]

    for chunk in (0, 1):
        for way in (0, 1):
            for step in range(1, REACH + 1):
                dp_copy(way, step, chunk).wait_send()
        for rel in range(3):
            pair_copy(rel, chunk).wait_send()
    for rel in range(3):
        loss_copy(rel).wait_send()
    sib_copy(0).wait_send()
    sib_copy(1).wait_send()
    z_copy.wait_send()


def local_part(student, teacher, band_codes):
    part, width = student.shape
    count = 4 * part
    slots = 2 * REACH + 1
    vmem = pl.BlockSpec(memory_space=pltpu.VMEM)
    anywhere = pl.BlockSpec(memory_space=pl.ANY)
    dma = pltpu.SemaphoreType.DMA
    return pl.pallas_call(
        kernel,
        out_shape=(
            jax.ShapeDtypeStruct((1, 1), jnp.float32),
            jax.ShapeDtypeStruct((part, width), jnp.float32),
        ),
        in_specs=[anywhere, anywhere, pl.BlockSpec(memory_space=pltpu.SMEM)],
        out_specs=(vmem, vmem),
        scratch_shapes=[
            pltpu.VMEM((2 * count, width), jnp.bfloat16),
            pltpu.VMEM((slots, 2 * part, width), jnp.bfloat16),
            pltpu.VMEM((2 * count, 128), jnp.float32),
            pltpu.VMEM((slots, 8, 2 * part), jnp.float32),
            pltpu.VMEM((2 * count, 2 * part), jnp.float32),
            pltpu.VMEM((count, 2 * part), jnp.bfloat16),
            pltpu.VMEM((count, width), jnp.float32),
            pltpu.VMEM((count, part), jnp.float32),
            pltpu.VMEM((4, 8, part), jnp.float32),
            pltpu.VMEM((3, 8, part), jnp.float32),
            pltpu.VMEM((2, part, width), jnp.float32),
            pltpu.VMEM((part, width), jnp.float32),
            pltpu.VMEM((part, width), jnp.float32),
            dma((2, 2)),
            dma((2, REACH, 2)),
            dma((2, REACH, 2)),
            dma((3, 2)),
            dma((3, 2)),
            dma((3,)),
            dma((3,)),
            dma((3,)),
            dma((3,)),
        ],
        compiler_params=pltpu.CompilerParams(
            collective_id=0, has_side_effects=True, vmem_limit_bytes=40 * 1024 * 1024
        ),
    )(student, teacher, band_codes)


def solution(mesh):
    return jax.shard_map(
        local_part,
        mesh=mesh,
        in_specs=(P(("dp", "pair"), None), P(("dp", "pair"), None), P()),
        out_specs=(P("dp", "pair"), P(("dp", "pair"), None)),
        check_vma=False,
    )
```

```python
import jax
import jax.numpy as jnp
from jax import lax
from jax.experimental import pallas as pl
from jax.experimental.pallas import tpu as pltpu
from jax.sharding import PartitionSpec as P

REACH = 3
ROW = 8
CHUNKS = 4
RELAYED = (1, 3)
LOG2E = 1.4426950408889634


def kernel(student, teacher, codes, loss_out, grad_out,
           bb, cbuf, hold, nb, nc, inner, ebuf, elast, acc, rows_acc, loss_acc, loss_in,
           got, z_out, z_in, r_out, r_in,
           local_sem, dp_send, dp_recv, hold_send, hold_recv, pair_send, pair_recv,
           fin_send, fin_recv, loss_send, loss_recv):
    n_dp = lax.axis_size("dp")
    part, width = student.shape
    count = 4 * part
    piece = 2 * part // CHUNKS
    bands = codes.shape[0]
    b = lax.axis_index("dp")
    p = lax.axis_index("pair")
    z_lo = p // 2
    core = p % 2
    sib = z_lo * 2 + (1 - core)
    zp = (1 - z_lo) * 2 + core
    diag = (1 - z_lo) * 2 + (1 - core)
    up = (b + 1) % n_dp
    down = (b + n_dp - 1) % n_dp
    column = b % ROW
    is_top = column == ROW - 1
    is_bottom = column == 0
    up_row = (b + ROW) % n_dp
    down_row = (b + n_dp - ROW) % n_dp
    row_bottom = b - column
    row_top = row_bottom + ROW - 1

    def dev(block, place):
        return {"dp": block, "pair": place}

    def rows_of(q, chunk):
        return pl.ds(pl.multiple_of(chunk * count + q * part, part), part)

    def quarter(q):
        return pl.ds(pl.multiple_of(q * part, part), part)

    barrier = pltpu.get_barrier_semaphore()

    def greet(*targets):
        for target in targets:
            pl.semaphore_signal(barrier, inc=1, device_id=target, device_id_type=pl.DeviceIdType.MESH)

    greet(dev(up, p), dev(down, p), dev(b, sib), dev(b, zp), dev(b, diag))

    @pl.when(is_top)
    def _():
        greet(dev(up_row, p), dev(down_row, p), dev(row_bottom, p))
        pl.semaphore_wait(barrier, 8)

    @pl.when(is_bottom)
    def _():
        greet(dev(up_row, p), dev(down_row, p), dev(row_top, p))
        pl.semaphore_wait(barrier, 8)

    @pl.when(jnp.logical_not(jnp.logical_or(is_top, is_bottom)))
    def _():
        pl.semaphore_wait(barrier, 5)

    own = (student, teacher)

    def remote(src, dst, ssem, rsem, target):
        return pltpu.make_async_remote_copy(
            src_ref=src, dst_ref=dst, send_sem=ssem, recv_sem=rsem,
            device_id=target, device_id_type=pl.DeviceIdType.MESH)

    def own_piece(chunk):
        first = chunk * piece
        return own[first // part].at[pl.ds(first % part, piece)]

    def slot_piece(slot, chunk):
        return cbuf.at[slot, pl.ds(chunk * piece, piece)]

    def dp_copy(way, step, chunk):
        sign = -1 if way == 0 else 1
        src = own_piece(chunk) if step == 1 else slot_piece(REACH + sign * (step - 1), chunk)
        return remote(src, slot_piece(REACH + sign * step, chunk),
                      dp_send.at[way, step - 1, chunk], dp_recv.at[way, step - 1, chunk],
                      dev(up if way == 0 else down, p))

    def hold_copy(way, step, chunk):
        sign = -1 if way == 0 else 1
        src = own_piece(chunk) if step == 1 else slot_piece(REACH + sign * (step - 1), chunk)
        index = RELAYED.index(chunk)
        return remote(src, hold.at[step - 1, index], dp_send.at[way, step - 1, chunk],
                      hold_recv.at[step - 1, index], dev(up_row if way == 0 else down_row, p))

    def pass_copy(way, step, chunk):
        sign = -1 if way == 0 else 1
        index = RELAYED.index(chunk)
        return remote(hold.at[step - 1, index], slot_piece(REACH + sign * step, chunk),
                      hold_send.at[step - 1, index], dp_recv.at[way, step - 1, chunk],
                      dev(row_bottom if way == 0 else row_top, p))

    def dp_start(way, step, chunk):
        if chunk in RELAYED:
            edge = is_top if way == 0 else is_bottom

            @pl.when(edge)
            def _():
                hold_copy(way, step, chunk).start()

            @pl.when(jnp.logical_not(edge))
            def _():
                dp_copy(way, step, chunk).start()
        else:
            dp_copy(way, step, chunk).start()

    def relay(step):
        for way in (0, 1):
            @pl.when(is_top if way == 0 else is_bottom)
            def _():
                for chunk in RELAYED:
                    hold_copy(way, step, chunk).wait_recv()
                    pass_copy(way, step, chunk).start()

    def pair_copy(rel, chunk):
        if rel == 2:
            src = dst = bb.at[rows_of(zp, chunk)]
        else:
            src, dst = own[chunk], bb.at[rows_of(p, chunk)]
        target = dev(b, zp if rel == 1 else sib)
        return remote(src, dst, pair_send.at[rel, chunk], pair_recv.at[rel, chunk], target)

    def pair_arrived(rel, chunk):
        q = (sib, zp, diag)[rel]
        ref = bb.at[rows_of(q, chunk)]
        remote(ref, ref, pair_send.at[rel, chunk], pair_recv.at[rel, chunk], dev(b, sib)).wait_recv()

    local = [pltpu.make_async_copy(own[c], cbuf.at[REACH, pl.ds(c * part, part)], local_sem.at[0, c]) for c in (0, 1)]
    local += [pltpu.make_async_copy(own[c], bb.at[rows_of(p, c)], local_sem.at[1, c]) for c in (0, 1)]
    for chunk in range(CHUNKS):
        for way in (0, 1):
            dp_start(way, 1, chunk)
        if chunk == 1:
            pair_copy(1, 0).start()
            pair_copy(0, 0).start()
    pair_copy(1, 1).start()
    pair_copy(0, 1).start()
    for c in local:
        c.start()

    scale = [2.0 / (codes[m].astype(jnp.float32) * width) for m in range(bands)]
    expo = [s * (-LOG2E) for s in scale]
    factor = 2.0 * width / count
    slope = [s * factor for s in scale]

    acc[...] = jnp.zeros_like(acc)
    rows_acc[...] = jnp.zeros_like(rows_acc)
    loss_acc[...] = jnp.zeros_like(loss_acc)

    def split_squares(x):
        sq = jnp.square(x.astype(jnp.float32))
        hi = sq.astype(jnp.bfloat16)
        lo = (sq - hi.astype(jnp.float32)).astype(jnp.bfloat16)
        return hi, lo

    def nt(x, y):
        return lax.dot_general(x, y, (((1,), (1,)), ((), ())), preferred_element_type=jnp.float32)

    def row_norms(q, chunk):
        here = rows_of(q, chunk)
        hi, lo = split_squares(bb[here, :])
        ones = jnp.ones((128, width), jnp.bfloat16)
        nb[here, :] = nt(hi, ones) + nt(lo, ones)

    step_rows = 32

    def work(offset, parts):
        slot = REACH + offset
        ahead = offset >= 0
        last = abs(offset) == REACH and parts == (1,)
        weight = [2.0 * w for w in slope] if offset == 0 else slope
        first = parts[0] * part
        wide = len(parts) * part
        here_cols = pl.ds(first, wide)
        cols = cbuf[slot, here_cols, :]
        hi, lo = split_squares(cols)
        ones = jnp.ones((8, width), jnp.bfloat16)
        nc[slot, :, here_cols] = nt(ones, hi) + nt(ones, lo)
        inner[pl.ds(0, count), here_cols] = nt(bb[pl.ds(0, count), :], cols)
        if ahead:
            inner[pl.ds(count, count), here_cols] = nt(bb[pl.ds(count, count), :], cols)

        def dist(here, at):
            norm = nb[here, :] + nc[slot, 0:1, pl.ds(at * part, part)]
            return norm - 2.0 * inner[here, pl.ds(at * part, part)]

        def sums(d, want_value, want_slope):
            value = slope_sum = None
            for m in range(bands):
                term = jnp.exp2(d * expo[m])
                if want_value:
                    value = term if value is None else value + term
                if want_slope:
                    scaled = term * weight[m]
                    slope_sum = scaled if slope_sum is None else slope_sum + scaled
            return value, slope_sum

        def fold(x):
            return jnp.sum(x.reshape(step_rows // 8, 8, part), axis=0)

        def body(i, total):
            here = pl.ds(pl.multiple_of(i * step_rows, step_rows), step_rows)
            there = pl.ds(pl.multiple_of(count + i * step_rows, step_rows), step_rows)
            for at in parts:
                value, coeff = sums(dist(here, at), ahead, True)
                if at == 0:
                    ebuf[here, pl.ds(0, part)] = coeff.astype(jnp.bfloat16)
                    rows_acc[here, :] -= coeff
                else:
                    negative = (-coeff).astype(jnp.bfloat16)
                    if last:
                        elast[here, pl.ds(0 if ahead else part, part)] = negative
                    else:
                        ebuf[here, pl.ds(part, part)] = negative
                    rows_acc[here, :] += coeff
                if ahead:
                    other, _ = sums(dist(there, at), True, False)
                    total = total + fold(value - other if at == 0 else other - value)
            return total

        total = lax.fori_loop(0, count // step_rows, body, jnp.zeros((8, part), jnp.float32))
        if ahead:
            loss_acc[offset] += total
        if not last:
            acc[...] += jnp.dot(ebuf[:, here_cols], cols, preferred_element_type=jnp.float32)

    def arrived(step, *chunks):
        for chunk in chunks:
            for way in (0, 1):
                dp_copy(way, step, chunk).wait_recv()
                if step < REACH:
                    dp_start(way, step + 1, chunk)

    for c in local:
        c.wait()
    for chunk in (0, 1):
        row_norms(p, chunk)
        pair_arrived(0, chunk)
        row_norms(sib, chunk)
    relay(1)
    arrived(1, 0, 1, 2, 3)
    for chunk in (0, 1):
        pair_arrived(1, chunk)
        pair_copy(2, chunk).start()
        row_norms(zp, chunk)
    for chunk in (0, 1):
        pair_arrived(2, chunk)
        row_norms(diag, chunk)
    ones = jnp.ones((8, count), jnp.bfloat16)
    centre = jnp.dot(ones, bb[pl.ds(0, count), :], preferred_element_type=jnp.float32)[0:1, :] * (1.0 / count)
    work(0, (0, 1))
    relay(2)
    work(1, (0, 1))
    arrived(2, 0, 1)
    work(-1, (0, 1))
    arrived(2, 2, 3)
    relay(3)
    work(2, (0, 1))
    work(-2, (0, 1))
    arrived(3, 0, 1)
    work(3, (0,))
    work(-3, (0,))
    arrived(3, 2, 3)
    work(3, (1,))
    work(-3, (1,))

    def loss_copy(rel):
        q = (sib, zp, diag)[rel]
        return remote(loss_acc.at[q], loss_in.at[rel], loss_send.at[rel], loss_recv.at[rel], dev(b, q))

    for rel in range(3):
        loss_copy(rel).start()

    tail = jnp.concatenate([cbuf[2 * REACH, pl.ds(part, part), :], cbuf[0, pl.ds(part, part), :]], axis=0)

    def gather_rows(q):
        here = quarter(q)
        products = acc[here, :] + jnp.dot(elast[here, :], tail, preferred_element_type=jnp.float32)
        return products, jnp.sum(rows_acc[here, :], axis=1, keepdims=True)

    def as_row(r):
        return jnp.transpose(jnp.broadcast_to(r, (part, 128)))[0:8, :]

    def sib_copy(which):
        q = (diag, sib)[which]
        return remote(acc.at[quarter(q)], got.at[which], fin_send.at[which], fin_recv.at[which], dev(b, sib))

    sib_row_copy = remote(r_out.at[0], r_in.at[0], fin_send.at[2], fin_recv.at[2], dev(b, sib))
    z_row_copy = remote(r_out.at[1], r_in.at[1], fin_send.at[3], fin_recv.at[3], dev(b, zp))
    z_copy = remote(z_out, z_in, fin_send.at[4], fin_recv.at[4], dev(b, zp))

    products, r = gather_rows(diag)
    acc[quarter(diag), :] = products + r * centre
    r_out[0] = as_row(r)
    sib_row_copy.start()
    sib_copy(0).start()
    products, r = gather_rows(zp)
    acc[quarter(zp), :] = products + r * centre
    r_out[1] = as_row(r)
    products, r = gather_rows(sib)
    acc[quarter(sib), :] = products + r * bb[quarter(sib), :].astype(jnp.float32)
    sib_copy(1).start()
    sib_row_copy.wait_recv()
    r_out[1] += r_in[0]
    z_row_copy.start()
    sib_copy(0).wait_recv()
    z_out[...] = (acc[quarter(zp), :] + got[0]).astype(jnp.bfloat16)
    z_copy.start()
    mine = bb[quarter(p), :].astype(jnp.float32)
    products, r = gather_rows(p)
    grad = products + r * mine
    for rel in range(3):
        loss_copy(rel).wait_recv()
    total = loss_acc[p] + loss_in[0] + loss_in[1] + loss_in[2]
    loss_out[...] = jnp.sum(jnp.sum(total, axis=1, keepdims=True), axis=0, keepdims=True) * (1.0 / count)
    sib_copy(1).wait_recv()
    z_row_copy.wait_recv()
    far = jnp.transpose(jnp.broadcast_to(r_in[1, 0:1, :], (128, part)))[:, 0:1]
    grad = grad + got[1] + far * (mine - centre)
    z_copy.wait_recv()
    grad_out[...] = grad + z_in[...].astype(jnp.float32)

    for chunk in range(CHUNKS):
        for way in (0, 1):
            for step in range(1, REACH + 1):
                dp_copy(way, step, chunk).wait_send()
    for way in (0, 1):
        @pl.when(is_top if way == 0 else is_bottom)
        def _():
            for step in range(1, REACH + 1):
                for chunk in RELAYED:
                    pass_copy(way, step, chunk).wait_send()
    for chunk in (0, 1):
        for rel in range(3):
            pair_copy(rel, chunk).wait_send()
    for rel in range(3):
        loss_copy(rel).wait_send()
    sib_copy(0).wait_send()
    sib_copy(1).wait_send()
    sib_row_copy.wait_send()
    z_row_copy.wait_send()
    z_copy.wait_send()


def local_part(student, teacher, band_codes):
    part, width = student.shape
    count = 4 * part
    slots = 2 * REACH + 1
    piece = 2 * part // CHUNKS
    relayed = len(RELAYED)
    vmem = pl.BlockSpec(memory_space=pltpu.VMEM)
    anywhere = pl.BlockSpec(memory_space=pl.ANY)
    dma = pltpu.SemaphoreType.DMA
    return pl.pallas_call(
        kernel,
        out_shape=(
            jax.ShapeDtypeStruct((1, 1), jnp.float32),
            jax.ShapeDtypeStruct((part, width), jnp.float32),
        ),
        in_specs=[anywhere, anywhere, pl.BlockSpec(memory_space=pltpu.SMEM)],
        out_specs=(vmem, vmem),
        scratch_shapes=[
            pltpu.VMEM((2 * count, width), jnp.bfloat16),
            pltpu.VMEM((slots, 2 * part, width), jnp.bfloat16),
            pltpu.VMEM((REACH, relayed, piece, width), jnp.bfloat16),
            pltpu.VMEM((2 * count, 128), jnp.float32),
            pltpu.VMEM((slots, 8, 2 * part), jnp.float32),
            pltpu.VMEM((2 * count, 2 * part), jnp.float32),
            pltpu.VMEM((count, 2 * part), jnp.bfloat16),
            pltpu.VMEM((count, 2 * part), jnp.bfloat16),
            pltpu.VMEM((count, width), jnp.float32),
            pltpu.VMEM((count, part), jnp.float32),
            pltpu.VMEM((REACH + 1, 8, part), jnp.float32),
            pltpu.VMEM((3, 8, part), jnp.float32),
            pltpu.VMEM((2, part, width), jnp.float32),
            pltpu.VMEM((part, width), jnp.bfloat16),
            pltpu.VMEM((part, width), jnp.bfloat16),
            pltpu.VMEM((2, 8, 128), jnp.float32),
            pltpu.VMEM((2, 8, 128), jnp.float32),
            dma((2, 2)),
            dma((2, REACH, CHUNKS)),
            dma((2, REACH, CHUNKS)),
            dma((REACH, relayed)),
            dma((REACH, relayed)),
            dma((3, 2)),
            dma((3, 2)),
            dma((5,)),
            dma((5,)),
            dma((3,)),
            dma((3,)),
        ],
        compiler_params=pltpu.CompilerParams(
            collective_id=0, has_side_effects=True, vmem_limit_bytes=60 * 1024 * 1024
        ),
    )(student, teacher, band_codes)


def solution(mesh):
    return jax.shard_map(
        local_part,
        mesh=mesh,
        in_specs=(P(("dp", "pair"), None), P(("dp", "pair"), None), P()),
        out_specs=(P("dp", "pair"), P(("dp", "pair"), None)),
        check_vma=False,
    )
```

```python
import jax
import jax.numpy as jnp
from jax import lax
from jax.experimental import pallas as pl
from jax.experimental.pallas import tpu as pltpu
from jax.sharding import PartitionSpec as P

REACH = 3
ROW = 8
CHUNKS = 4
RELAYED = (1, 3)
SIDE = (0, 1)
LOG2E = 1.4426950408889634


def kernel(student, teacher, codes, loss_out, grad_out,
           bb, cbuf, hold, side_hold, nb, nc, inner, ebuf, elast, acc, rows_acc, loss_acc, loss_in,
           got, z_out, z_in, r_out, r_in,
           local_sem, dp_send, dp_recv, hold_send, hold_recv, side_send, side_recv, side_pass, pair_send, pair_recv,
           fin_send, fin_recv, loss_send, loss_recv):
    n_dp = lax.axis_size("dp")
    part, width = student.shape
    count = 4 * part
    piece = 2 * part // CHUNKS
    bands = codes.shape[0]
    b = lax.axis_index("dp")
    p = lax.axis_index("pair")
    z_lo = p // 2
    core = p % 2
    sib = z_lo * 2 + (1 - core)
    zp = (1 - z_lo) * 2 + core
    diag = (1 - z_lo) * 2 + (1 - core)
    up = (b + 1) % n_dp
    down = (b + n_dp - 1) % n_dp
    column = b % ROW
    is_top = column == ROW - 1
    is_bottom = column == 0
    up_row = (b + ROW) % n_dp
    down_row = (b + n_dp - ROW) % n_dp
    row_bottom = b - column
    row_top = row_bottom + ROW - 1

    def dev(block, place):
        return {"dp": block, "pair": place}

    def rows_of(q, chunk):
        return pl.ds(pl.multiple_of(chunk * count + q * part, part), part)

    def quarter(q):
        return pl.ds(pl.multiple_of(q * part, part), part)

    barrier = pltpu.get_barrier_semaphore()

    def greet(*targets):
        for target in targets:
            pl.semaphore_signal(barrier, inc=1, device_id=target, device_id_type=pl.DeviceIdType.MESH)

    greet(dev(up, p), dev(down, p), dev(b, sib), dev(b, zp), dev(b, diag))
    near_top = column == ROW - 2
    near_bottom = column == 1
    is_edge = jnp.logical_or(is_top, is_bottom)
    is_next = jnp.logical_or(near_top, near_bottom)

    @pl.when(is_top)
    def _():
        greet(dev(up_row, p), dev(down_row, p), dev(row_bottom, p), dev(row_bottom + 1, p))
        pl.semaphore_wait(barrier, 9)

    @pl.when(is_bottom)
    def _():
        greet(dev(up_row, p), dev(down_row, p), dev(row_top, p), dev(row_top - 1, p))
        pl.semaphore_wait(barrier, 9)

    @pl.when(near_top)
    def _():
        greet(dev(up_row, p), dev(down_row, p), dev(row_bottom, p))
        pl.semaphore_wait(barrier, 8)

    @pl.when(near_bottom)
    def _():
        greet(dev(up_row, p), dev(down_row, p), dev(row_top, p))
        pl.semaphore_wait(barrier, 8)

    @pl.when(jnp.logical_not(jnp.logical_or(is_edge, is_next)))
    def _():
        pl.semaphore_wait(barrier, 5)

    own = (student, teacher)

    def remote(src, dst, ssem, rsem, target):
        return pltpu.make_async_remote_copy(
            src_ref=src, dst_ref=dst, send_sem=ssem, recv_sem=rsem,
            device_id=target, device_id_type=pl.DeviceIdType.MESH)

    def own_piece(chunk):
        first = chunk * piece
        return own[first // part].at[pl.ds(first % part, piece)]

    def slot_piece(slot, chunk):
        return cbuf.at[slot, pl.ds(chunk * piece, piece)]

    def dp_copy(way, step, chunk):
        sign = -1 if way == 0 else 1
        src = own_piece(chunk) if step == 1 else slot_piece(REACH + sign * (step - 1), chunk)
        return remote(src, slot_piece(REACH + sign * step, chunk),
                      dp_send.at[way, step - 1, chunk], dp_recv.at[way, step - 1, chunk],
                      dev(up if way == 0 else down, p))

    def hold_copy(way, step, chunk):
        sign = -1 if way == 0 else 1
        src = own_piece(chunk) if step == 1 else slot_piece(REACH + sign * (step - 1), chunk)
        index = RELAYED.index(chunk)
        return remote(src, hold.at[step - 1, index], dp_send.at[way, step - 1, chunk],
                      hold_recv.at[step - 1, index], dev(up_row if way == 0 else down_row, p))

    def pass_copy(way, step, chunk):
        sign = -1 if way == 0 else 1
        index = RELAYED.index(chunk)
        return remote(hold.at[step - 1, index], slot_piece(REACH + sign * step, chunk),
                      hold_send.at[step - 1, index], dp_recv.at[way, step - 1, chunk],
                      dev(row_bottom if way == 0 else row_top, p))

    def side_copy(way, chunk):
        sign = -1 if way == 0 else 1
        index = SIDE.index(chunk)
        return remote(slot_piece(REACH + sign, chunk), side_hold.at[index], side_send.at[index], side_recv.at[index],
                      dev(up_row if way == 0 else down_row, p))

    def side_pass_copy(way, chunk):
        sign = -1 if way == 0 else 1
        index = SIDE.index(chunk)
        return remote(side_hold.at[index], slot_piece(REACH + sign * REACH, chunk), side_pass.at[index],
                      dp_recv.at[way, REACH - 1, chunk], dev(row_bottom if way == 0 else row_top, p))

    def dp_start(way, step, chunk):
        edge = is_top if way == 0 else is_bottom
        by_side = step == REACH and chunk in SIDE
        if by_side or chunk in RELAYED:
            if not by_side:
                @pl.when(edge)
                def _():
                    hold_copy(way, step, chunk).start()

            @pl.when(jnp.logical_not(edge))
            def _():
                dp_copy(way, step, chunk).start()
        else:
            dp_copy(way, step, chunk).start()

    def relay(way, step, *chunks):
        for chunk in chunks:
            hold_copy(way, step, chunk).wait_recv()
            pass_copy(way, step, chunk).start()

    def side_relay(way):
        for chunk in SIDE:
            side_copy(way, chunk).wait_recv()
            side_pass_copy(way, chunk).start()

    def take(way, step, *chunks):
        for chunk in chunks:
            dp_copy(way, step, chunk).wait_recv()
            if step < REACH:
                dp_start(way, step + 1, chunk)

    high = column >= ROW // 2
    everything = tuple(range(CHUNKS))
    straight = tuple(c for c in everything if c not in RELAYED)
    relayed_last = tuple(c for c in RELAYED if c not in SIDE)

    def by_kind(edge_order, next_order, inner_order):
        for near in (0, 1):
            far = 1 - near
            for chosen, order in ((is_edge, edge_order), (is_next, next_order),
                                  (jnp.logical_not(jnp.logical_or(is_edge, is_next)), inner_order)):
                @pl.when(jnp.logical_and(chosen, high if near == 0 else jnp.logical_not(high)))
                def _():
                    order(near, far)

    def edge_first(near, far):
        take(near, 1, 0, 1)
        relay(near, 1, RELAYED[0])
        take(near, 1, 2, 3)
        relay(near, 1, RELAYED[1])
        take(far, 1, *straight)

    def next_first(near, far):
        for chunk in everything:
            take(near, 1, chunk)
            if chunk in SIDE:
                side_copy(near, chunk).start()
            take(far, 1, chunk)

    def inner_first(near, far):
        for chunk in everything:
            take(near, 1, chunk)
            take(far, 1, chunk)

    def edge_second(near, far):
        take(far, 1, *RELAYED)

    def next_second(near, far):
        side_relay(near)

    def nothing(near, far):
        pass

    def edge_third(near, far):
        take(near, 2, 0, 1)
        relay(near, 2, RELAYED[0])
        take(near, 2, 2, 3)
        relay(near, 2, RELAYED[1])

    def inner_third(near, far):
        take(near, 2, *everything)

    def edge_fourth(near, far):
        take(far, 2, *straight)
        take(far, 2, *RELAYED)
        relay(near, 3, *relayed_last)

    def inner_fourth(near, far):
        take(far, 2, *everything)

    def pair_copy(rel, chunk):
        if rel == 2:
            src = dst = bb.at[rows_of(zp, chunk)]
        else:
            src, dst = own[chunk], bb.at[rows_of(p, chunk)]
        target = dev(b, zp if rel == 1 else sib)
        return remote(src, dst, pair_send.at[rel, chunk], pair_recv.at[rel, chunk], target)

    def pair_arrived(rel, chunk):
        q = (sib, zp, diag)[rel]
        ref = bb.at[rows_of(q, chunk)]
        remote(ref, ref, pair_send.at[rel, chunk], pair_recv.at[rel, chunk], dev(b, sib)).wait_recv()

    local = [pltpu.make_async_copy(own[c], cbuf.at[REACH, pl.ds(c * part, part)], local_sem.at[0, c]) for c in (0, 1)]
    local += [pltpu.make_async_copy(own[c], bb.at[rows_of(p, c)], local_sem.at[1, c]) for c in (0, 1)]
    for chunk in range(CHUNKS):
        for way in (0, 1):
            dp_start(way, 1, chunk)
        if chunk == 1:
            pair_copy(1, 0).start()
            pair_copy(0, 0).start()
    pair_copy(1, 1).start()
    pair_copy(0, 1).start()
    for c in local:
        c.start()

    scale = [2.0 / (codes[m].astype(jnp.float32) * width) for m in range(bands)]
    expo = [s * (-LOG2E) for s in scale]
    factor = 2.0 * width / count
    slope = [s * factor for s in scale]

    acc[...] = jnp.zeros_like(acc)
    rows_acc[...] = jnp.zeros_like(rows_acc)
    loss_acc[...] = jnp.zeros_like(loss_acc)

    def split_squares(x):
        sq = jnp.square(x.astype(jnp.float32))
        hi = sq.astype(jnp.bfloat16)
        lo = (sq - hi.astype(jnp.float32)).astype(jnp.bfloat16)
        return hi, lo

    def nt(x, y):
        return lax.dot_general(x, y, (((1,), (1,)), ((), ())), preferred_element_type=jnp.float32)

    def row_norms(q, chunk):
        here = rows_of(q, chunk)
        hi, lo = split_squares(bb[here, :])
        ones = jnp.ones((128, width), jnp.bfloat16)
        nb[here, :] = nt(hi, ones) + nt(lo, ones)

    step_rows = 32

    def col_norms(offset, parts):
        slot = REACH + offset
        here = pl.ds(parts[0] * part, len(parts) * part)
        hi, lo = split_squares(cbuf[slot, here, :])
        ones = jnp.ones((8, width), jnp.bfloat16)
        nc[slot, :, here] = nt(ones, hi) + nt(ones, lo)

    chip_rows = 2 * part

    def work(offset, parts, chip=None):
        slot = REACH + offset
        ahead = offset >= 0
        last = abs(offset) == REACH and parts == (1,)
        weight = [2.0 * w for w in slope] if offset == 0 else slope
        here_cols = pl.ds(parts[0] * part, len(parts) * part)
        if chip is None:
            base, rows = 0, count
        else:
            base, rows = (z_lo if chip == 0 else 1 - z_lo) * chip_rows, chip_rows
        if chip != 1:
            col_norms(offset, parts)
        cols = cbuf[slot, here_cols, :]

        def block(first, size):
            return pl.ds(pl.multiple_of(base + first, size), size)

        inner[pl.ds(0, rows), here_cols] = nt(bb[block(0, rows), :], cols)
        if ahead:
            inner[pl.ds(count, rows), here_cols] = nt(bb[block(count, rows), :], cols)

        def dist(norm_rows, here, at):
            norm = nb[norm_rows, :] + nc[slot, 0:1, pl.ds(at * part, part)]
            return norm - 2.0 * inner[here, pl.ds(at * part, part)]

        def sums(d, want_value, want_slope):
            value = slope_sum = None
            for m in range(bands):
                term = jnp.exp2(d * expo[m])
                if want_value:
                    value = term if value is None else value + term
                if want_slope:
                    scaled = term * weight[m]
                    slope_sum = scaled if slope_sum is None else slope_sum + scaled
            return value, slope_sum

        def fold(x):
            return jnp.sum(x.reshape(step_rows // 8, 8, part), axis=0)

        def body(i, total):
            here = pl.ds(pl.multiple_of(i * step_rows, step_rows), step_rows)
            there = pl.ds(pl.multiple_of(count + i * step_rows, step_rows), step_rows)
            block_here = block(i * step_rows, step_rows)
            block_there = block(count + i * step_rows, step_rows)
            for at in parts:
                value, coeff = sums(dist(block_here, here, at), ahead, True)
                if at == 0:
                    ebuf[here, pl.ds(0, part)] = coeff.astype(jnp.bfloat16)
                    rows_acc[block_here, :] -= coeff
                else:
                    negative = (-coeff).astype(jnp.bfloat16)
                    if last:
                        elast[here, :] = negative
                    else:
                        ebuf[here, pl.ds(part, part)] = negative
                    rows_acc[block_here, :] += coeff
                if ahead:
                    other, _ = sums(dist(block_there, there, at), True, False)
                    total = total + fold(value - other if at == 0 else other - value)
            return total

        total = lax.fori_loop(0, rows // step_rows, body, jnp.zeros((8, part), jnp.float32))
        if ahead:
            loss_acc[offset] += total
        if not last:
            acc[block(0, rows), :] += jnp.dot(
                ebuf[pl.ds(0, rows), here_cols], cols, preferred_element_type=jnp.float32)

    for c in local:
        c.wait()
    for chunk in (0, 1):
        row_norms(p, chunk)
        pair_arrived(0, chunk)
        row_norms(sib, chunk)
    both = (0, 1)
    by_kind(edge_first, next_first, inner_first)
    work(0, both, 0)
    by_kind(edge_second, next_second, nothing)
    work(1, both, 0)
    work(-1, both, 0)
    by_kind(edge_third, inner_third, inner_third)
    for chunk in (0, 1):
        pair_arrived(1, chunk)
        pair_copy(2, chunk).start()
        row_norms(zp, chunk)
    ones = jnp.ones((8, count), jnp.bfloat16)
    for chunk in (0, 1):
        pair_arrived(2, chunk)
        row_norms(diag, chunk)
    centre = jnp.dot(ones, bb[pl.ds(0, count), :], preferred_element_type=jnp.float32)[0:1, :] * (1.0 / count)
    work(0, both, 1)
    work(1, both, 1)
    work(-1, both, 1)
    by_kind(edge_fourth, inner_fourth, inner_fourth)
    work(2, both)
    work(-2, both)
    for near in (0, 1):
        @pl.when(high if near == 0 else jnp.logical_not(high))
        def _():
            near_offset = -REACH if near == 0 else REACH
            take(near, REACH, *everything)
            work(near_offset, both)
            take(1 - near, REACH, 0, 1)
            work(-near_offset, (0,))
            take(1 - near, REACH, 2, 3)
            work(-near_offset, (1,))

    def loss_copy(rel):
        q = (sib, zp, diag)[rel]
        return remote(loss_acc.at[q], loss_in.at[rel], loss_send.at[rel], loss_recv.at[rel], dev(b, q))

    for rel in range(3):
        loss_copy(rel).start()

    tail = cbuf[jnp.where(high, 2 * REACH, 0), pl.ds(part, part), :]

    def gather_rows(q):
        here = quarter(q)
        products = acc[here, :] + jnp.dot(elast[here, :], tail, preferred_element_type=jnp.float32)
        return products, jnp.sum(rows_acc[here, :], axis=1, keepdims=True)

    def as_row(r):
        return jnp.transpose(jnp.broadcast_to(r, (part, 128)))[0:8, :]

    def sib_copy(which):
        q = (diag, sib)[which]
        return remote(acc.at[quarter(q)], got.at[which], fin_send.at[which], fin_recv.at[which], dev(b, sib))

    sib_row_copy = remote(r_out.at[0], r_in.at[0], fin_send.at[2], fin_recv.at[2], dev(b, sib))
    z_row_copy = remote(r_out.at[1], r_in.at[1], fin_send.at[3], fin_recv.at[3], dev(b, zp))
    z_copy = remote(z_out, z_in, fin_send.at[4], fin_recv.at[4], dev(b, zp))

    products, r = gather_rows(diag)
    acc[quarter(diag), :] = products + r * centre
    r_out[0] = as_row(r)
    sib_row_copy.start()
    sib_copy(0).start()
    products, r = gather_rows(zp)
    acc[quarter(zp), :] = products + r * centre
    r_out[1] = as_row(r)
    products, r = gather_rows(sib)
    acc[quarter(sib), :] = products + r * bb[quarter(sib), :].astype(jnp.float32)
    sib_copy(1).start()
    sib_row_copy.wait_recv()
    r_out[1] += r_in[0]
    z_row_copy.start()
    sib_copy(0).wait_recv()
    z_out[...] = (acc[quarter(zp), :] + got[0]).astype(jnp.bfloat16)
    z_copy.start()
    mine = bb[quarter(p), :].astype(jnp.float32)
    products, r = gather_rows(p)
    grad = products + r * mine
    for rel in range(3):
        loss_copy(rel).wait_recv()
    total = loss_acc[p] + loss_in[0] + loss_in[1] + loss_in[2]
    loss_out[...] = jnp.sum(jnp.sum(total, axis=1, keepdims=True), axis=0, keepdims=True) * (1.0 / count)
    sib_copy(1).wait_recv()
    z_row_copy.wait_recv()
    far = jnp.transpose(jnp.broadcast_to(r_in[1, 0:1, :], (128, part)))[:, 0:1]
    grad = grad + got[1] + far * (mine - centre)
    z_copy.wait_recv()
    grad_out[...] = grad + z_in[...].astype(jnp.float32)

    for chunk in range(CHUNKS):
        for way in (0, 1):
            for step in range(1, REACH + 1):
                if step == REACH and chunk in SIDE:
                    @pl.when(jnp.logical_not(is_top if way == 0 else is_bottom))
                    def _():
                        dp_copy(way, step, chunk).wait_send()
                else:
                    dp_copy(way, step, chunk).wait_send()
    for way in (0, 1):
        @pl.when(is_top if way == 0 else is_bottom)
        def _():
            for step in range(1, REACH + 1):
                for chunk in RELAYED if step < REACH else relayed_last:
                    pass_copy(way, step, chunk).wait_send()

        @pl.when(near_top if way == 0 else near_bottom)
        def _():
            for chunk in SIDE:
                side_copy(way, chunk).wait_send()
                side_pass_copy(way, chunk).wait_send()
    for chunk in (0, 1):
        for rel in range(3):
            pair_copy(rel, chunk).wait_send()
    for rel in range(3):
        loss_copy(rel).wait_send()
    sib_copy(0).wait_send()
    sib_copy(1).wait_send()
    sib_row_copy.wait_send()
    z_row_copy.wait_send()
    z_copy.wait_send()


def local_part(student, teacher, band_codes):
    part, width = student.shape
    count = 4 * part
    slots = 2 * REACH + 1
    piece = 2 * part // CHUNKS
    relayed = len(RELAYED)
    vmem = pl.BlockSpec(memory_space=pltpu.VMEM)
    anywhere = pl.BlockSpec(memory_space=pl.ANY)
    dma = pltpu.SemaphoreType.DMA
    return pl.pallas_call(
        kernel,
        out_shape=(
            jax.ShapeDtypeStruct((1, 1), jnp.float32),
            jax.ShapeDtypeStruct((part, width), jnp.float32),
        ),
        in_specs=[anywhere, anywhere, pl.BlockSpec(memory_space=pltpu.SMEM)],
        out_specs=(vmem, vmem),
        scratch_shapes=[
            pltpu.VMEM((2 * count, width), jnp.bfloat16),
            pltpu.VMEM((slots, 2 * part, width), jnp.bfloat16),
            pltpu.VMEM((REACH, relayed, piece, width), jnp.bfloat16),
            pltpu.VMEM((len(SIDE), piece, width), jnp.bfloat16),
            pltpu.VMEM((2 * count, 128), jnp.float32),
            pltpu.VMEM((slots, 8, 2 * part), jnp.float32),
            pltpu.VMEM((2 * count, 2 * part), jnp.float32),
            pltpu.VMEM((count, 2 * part), jnp.bfloat16),
            pltpu.VMEM((count, part), jnp.bfloat16),
            pltpu.VMEM((count, width), jnp.float32),
            pltpu.VMEM((count, part), jnp.float32),
            pltpu.VMEM((REACH + 1, 8, part), jnp.float32),
            pltpu.VMEM((3, 8, part), jnp.float32),
            pltpu.VMEM((2, part, width), jnp.float32),
            pltpu.VMEM((part, width), jnp.bfloat16),
            pltpu.VMEM((part, width), jnp.bfloat16),
            pltpu.VMEM((2, 8, 128), jnp.float32),
            pltpu.VMEM((2, 8, 128), jnp.float32),
            dma((2, 2)),
            dma((2, REACH, CHUNKS)),
            dma((2, REACH, CHUNKS)),
            dma((REACH, relayed)),
            dma((REACH, relayed)),
            dma((len(SIDE),)),
            dma((len(SIDE),)),
            dma((len(SIDE),)),
            dma((3, 2)),
            dma((3, 2)),
            dma((5,)),
            dma((5,)),
            dma((3,)),
            dma((3,)),
        ],
        compiler_params=pltpu.CompilerParams(
            collective_id=0, has_side_effects=True, vmem_limit_bytes=60 * 1024 * 1024
        ),
    )(student, teacher, band_codes)


def solution(mesh):
    return jax.shard_map(
        local_part,
        mesh=mesh,
        in_specs=(P(("dp", "pair"), None), P(("dp", "pair"), None), P()),
        out_specs=(P("dp", "pair"), P(("dp", "pair"), None)),
        check_vma=False,
    )
```

```python
import jax
import jax.numpy as jnp
from jax import lax
from jax.experimental import pallas as pl
from jax.experimental.pallas import tpu as pltpu
from jax.sharding import PartitionSpec as P

REACH = 3
ROW = 8
CHUNKS = 4
RELAYED = (1, 3)
SIDE = (0, 1)
LOG2E = 1.4426950408889634


def kernel(student, teacher, codes, loss_out, grad_out,
           bb, cbuf, hold, side_hold, nb, nc, inner, ebuf, elast, acc, rows_acc, loss_acc, loss_in,
           got, z_out, z_in, r_out, r_in,
           local_sem, dp_send, dp_recv, hold_send, hold_recv, side_send, side_recv, side_pass, pair_send, pair_recv,
           fin_send, fin_recv, loss_send, loss_recv):
    n_dp = lax.axis_size("dp")
    part, width = student.shape
    count = 4 * part
    piece = 2 * part // CHUNKS
    bands = codes.shape[0]
    b = lax.axis_index("dp")
    p = lax.axis_index("pair")
    z_lo = p // 2
    core = p % 2
    sib = z_lo * 2 + (1 - core)
    zp = (1 - z_lo) * 2 + core
    diag = (1 - z_lo) * 2 + (1 - core)
    up = (b + 1) % n_dp
    down = (b + n_dp - 1) % n_dp
    column = b % ROW
    is_top = column == ROW - 1
    is_bottom = column == 0
    up_row = (b + ROW) % n_dp
    down_row = (b + n_dp - ROW) % n_dp
    row_bottom = b - column
    row_top = row_bottom + ROW - 1

    def dev(block, place):
        return {"dp": block, "pair": place}

    def rows_of(q, chunk):
        return pl.ds(pl.multiple_of(chunk * count + q * part, part), part)

    def quarter(q):
        return pl.ds(pl.multiple_of(q * part, part), part)

    barrier = pltpu.get_barrier_semaphore()

    def greet(*targets):
        for target in targets:
            pl.semaphore_signal(barrier, inc=1, device_id=target, device_id_type=pl.DeviceIdType.MESH)

    greet(dev(up, p), dev(down, p), dev(b, sib), dev(b, zp), dev(b, diag))
    near_top = column == ROW - 2
    near_bottom = column == 1
    is_edge = jnp.logical_or(is_top, is_bottom)
    is_next = jnp.logical_or(near_top, near_bottom)

    @pl.when(is_top)
    def _():
        greet(dev(up_row, p), dev(down_row, p), dev(row_bottom, p), dev(row_bottom + 1, p))
        pl.semaphore_wait(barrier, 9)

    @pl.when(is_bottom)
    def _():
        greet(dev(up_row, p), dev(down_row, p), dev(row_top, p), dev(row_top - 1, p))
        pl.semaphore_wait(barrier, 9)

    @pl.when(near_top)
    def _():
        greet(dev(up_row, p), dev(down_row, p), dev(row_bottom, p))
        pl.semaphore_wait(barrier, 8)

    @pl.when(near_bottom)
    def _():
        greet(dev(up_row, p), dev(down_row, p), dev(row_top, p))
        pl.semaphore_wait(barrier, 8)

    @pl.when(jnp.logical_not(jnp.logical_or(is_edge, is_next)))
    def _():
        pl.semaphore_wait(barrier, 5)

    own = (student, teacher)

    def remote(src, dst, ssem, rsem, target):
        return pltpu.make_async_remote_copy(
            src_ref=src, dst_ref=dst, send_sem=ssem, recv_sem=rsem,
            device_id=target, device_id_type=pl.DeviceIdType.MESH)

    def own_piece(chunk):
        first = chunk * piece
        return own[first // part].at[pl.ds(first % part, piece)]

    def slot_piece(slot, chunk):
        return cbuf.at[slot, pl.ds(chunk * piece, piece)]

    def dp_copy(way, step, chunk):
        sign = -1 if way == 0 else 1
        src = own_piece(chunk) if step == 1 else slot_piece(REACH + sign * (step - 1), chunk)
        return remote(src, slot_piece(REACH + sign * step, chunk),
                      dp_send.at[way, step - 1, chunk], dp_recv.at[way, step - 1, chunk],
                      dev(up if way == 0 else down, p))

    def hold_copy(way, step, chunk):
        sign = -1 if way == 0 else 1
        src = own_piece(chunk) if step == 1 else slot_piece(REACH + sign * (step - 1), chunk)
        index = RELAYED.index(chunk)
        return remote(src, hold.at[step - 1, index], dp_send.at[way, step - 1, chunk],
                      hold_recv.at[step - 1, index], dev(up_row if way == 0 else down_row, p))

    def pass_copy(way, step, chunk):
        sign = -1 if way == 0 else 1
        index = RELAYED.index(chunk)
        return remote(hold.at[step - 1, index], slot_piece(REACH + sign * step, chunk),
                      hold_send.at[step - 1, index], dp_recv.at[way, step - 1, chunk],
                      dev(row_bottom if way == 0 else row_top, p))

    def side_copy(way, chunk):
        sign = -1 if way == 0 else 1
        index = SIDE.index(chunk)
        return remote(slot_piece(REACH + sign, chunk), side_hold.at[index], side_send.at[index], side_recv.at[index],
                      dev(up_row if way == 0 else down_row, p))

    def side_pass_copy(way, chunk):
        sign = -1 if way == 0 else 1
        index = SIDE.index(chunk)
        return remote(side_hold.at[index], slot_piece(REACH + sign * REACH, chunk), side_pass.at[index],
                      dp_recv.at[way, REACH - 1, chunk], dev(row_bottom if way == 0 else row_top, p))

    def dp_start(way, step, chunk):
        edge = is_top if way == 0 else is_bottom
        by_side = step == REACH and chunk in SIDE
        if by_side or chunk in RELAYED:
            if not by_side:
                @pl.when(edge)
                def _():
                    hold_copy(way, step, chunk).start()

            @pl.when(jnp.logical_not(edge))
            def _():
                dp_copy(way, step, chunk).start()
        else:
            dp_copy(way, step, chunk).start()

    def relay(way, step, *chunks):
        for chunk in chunks:
            hold_copy(way, step, chunk).wait_recv()
            pass_copy(way, step, chunk).start()

    def side_relay(way):
        for chunk in SIDE:
            side_copy(way, chunk).wait_recv()
            side_pass_copy(way, chunk).start()

    def take(way, step, *chunks):
        for chunk in chunks:
            dp_copy(way, step, chunk).wait_recv()
            if step < REACH:
                dp_start(way, step + 1, chunk)

    high = column >= ROW // 2
    everything = tuple(range(CHUNKS))
    straight = tuple(c for c in everything if c not in RELAYED)
    relayed_last = tuple(c for c in RELAYED if c not in SIDE)

    def by_kind(edge_order, next_order, inner_order):
        for near in (0, 1):
            far = 1 - near
            for chosen, order in ((is_edge, edge_order), (is_next, next_order),
                                  (jnp.logical_not(jnp.logical_or(is_edge, is_next)), inner_order)):
                @pl.when(jnp.logical_and(chosen, high if near == 0 else jnp.logical_not(high)))
                def _():
                    order(near, far)

    def edge_first(near, far):
        take(near, 1, 0, 1)
        relay(near, 1, RELAYED[0])
        take(near, 1, 2, 3)
        relay(near, 1, RELAYED[1])
        take(far, 1, *straight)

    def next_first(near, far):
        for chunk in everything:
            take(near, 1, chunk)
            take(far, 1, chunk)
        for chunk in SIDE:
            side_copy(near, chunk).start()

    def inner_first(near, far):
        for chunk in everything:
            take(near, 1, chunk)
            take(far, 1, chunk)

    def edge_second(near, far):
        take(far, 1, *RELAYED)

    def next_second(near, far):
        side_relay(near)

    def nothing(near, far):
        pass

    def edge_third(near, far):
        take(near, 2, 0, 1)
        relay(near, 2, RELAYED[0])
        take(near, 2, 2, 3)
        relay(near, 2, RELAYED[1])

    def next_third(near, far):
        take(near, 2, *everything)

    def inner_third(near, far):
        for chunk in everything:
            take(near, 2, chunk)
            take(far, 2, chunk)

    def edge_fourth(near, far):
        take(far, 2, *straight)

    def edge_fifth(near, far):
        take(far, 2, *RELAYED)

    def edge_sixth(near, far):
        relay(near, 3, *relayed_last)

    def next_fourth(near, far):
        take(far, 2, *everything)

    def pair_copy(rel, chunk):
        if rel == 2:
            src = dst = bb.at[rows_of(zp, chunk)]
        else:
            src, dst = own[chunk], bb.at[rows_of(p, chunk)]
        target = dev(b, zp if rel == 1 else sib)
        return remote(src, dst, pair_send.at[rel, chunk], pair_recv.at[rel, chunk], target)

    def pair_arrived(rel, chunk):
        q = (sib, zp, diag)[rel]
        ref = bb.at[rows_of(q, chunk)]
        remote(ref, ref, pair_send.at[rel, chunk], pair_recv.at[rel, chunk], dev(b, sib)).wait_recv()

    local = [pltpu.make_async_copy(own[c], cbuf.at[REACH, pl.ds(c * part, part)], local_sem.at[0, c]) for c in (0, 1)]
    local += [pltpu.make_async_copy(own[c], bb.at[rows_of(p, c)], local_sem.at[1, c]) for c in (0, 1)]
    for chunk in range(CHUNKS):
        for way in (0, 1):
            dp_start(way, 1, chunk)
        if chunk == 1:
            pair_copy(1, 0).start()
            pair_copy(0, 0).start()
    pair_copy(1, 1).start()
    pair_copy(0, 1).start()
    for c in local:
        c.start()

    scale = [2.0 / (codes[m].astype(jnp.float32) * width) for m in range(bands)]
    expo = [s * (-LOG2E) for s in scale]
    factor = 2.0 * width / count
    slope = [s * factor for s in scale]

    acc[...] = jnp.zeros_like(acc)
    rows_acc[...] = jnp.zeros_like(rows_acc)
    loss_acc[...] = jnp.zeros_like(loss_acc)

    def split_squares(x):
        sq = jnp.square(x.astype(jnp.float32))
        hi = sq.astype(jnp.bfloat16)
        lo = (sq - hi.astype(jnp.float32)).astype(jnp.bfloat16)
        return hi, lo

    def nt(x, y):
        return lax.dot_general(x, y, (((1,), (1,)), ((), ())), preferred_element_type=jnp.float32)

    def row_norms(q, chunk):
        here = rows_of(q, chunk)
        hi, lo = split_squares(bb[here, :])
        ones = jnp.ones((128, width), jnp.bfloat16)
        nb[here, :] = nt(hi, ones) + nt(lo, ones)

    step_rows = 128

    def col_norms(offset, parts):
        slot = REACH + offset
        here = pl.ds(parts[0] * part, len(parts) * part)
        sq = jnp.square(cbuf[slot, here, :].astype(jnp.float32))
        folded = sq[:, 0:128]
        for k in range(1, width // 128):
            folded = folded + sq[:, k * 128:(k + 1) * 128]
        norms = jnp.sum(jnp.transpose(folded), axis=0, keepdims=True)
        nc[slot, :, here] = jnp.broadcast_to(norms, (8, len(parts) * part))

    chip_rows = 2 * part

    def work(offset, parts, chip=None):
        slot = REACH + offset
        ahead = offset >= 0
        last = abs(offset) == REACH and parts == (1,)
        weight = [2.0 * w for w in slope] if offset == 0 else slope
        here_cols = pl.ds(parts[0] * part, len(parts) * part)
        if chip is None:
            base, rows = 0, count
        else:
            base, rows = (z_lo if chip == 0 else 1 - z_lo) * chip_rows, chip_rows
        if chip != 1:
            col_norms(offset, parts)
        cols = cbuf[slot, here_cols, :]

        def block(first, size):
            return pl.ds(pl.multiple_of(base + first, size), size)

        inner[pl.ds(0, rows), here_cols] = nt(bb[block(0, rows), :], cols)
        if ahead:
            inner[pl.ds(count, rows), here_cols] = nt(bb[block(count, rows), :], cols)

        def dist(norm_rows, here, at):
            norm = nb[norm_rows, :] + nc[slot, 0:1, pl.ds(at * part, part)]
            return norm - 2.0 * inner[here, pl.ds(at * part, part)]

        def sums(d, want_value, want_slope):
            value = slope_sum = None
            for m in range(bands):
                term = jnp.exp2(d * expo[m])
                if want_value:
                    value = term if value is None else value + term
                if want_slope:
                    scaled = term * weight[m]
                    slope_sum = scaled if slope_sum is None else slope_sum + scaled
            return value, slope_sum

        def fold(x):
            return jnp.sum(x.reshape(step_rows // 8, 8, part), axis=0)

        def body(i, total):
            here = pl.ds(pl.multiple_of(i * step_rows, step_rows), step_rows)
            there = pl.ds(pl.multiple_of(count + i * step_rows, step_rows), step_rows)
            block_here = block(i * step_rows, step_rows)
            block_there = block(count + i * step_rows, step_rows)
            for at in parts:
                value, coeff = sums(dist(block_here, here, at), ahead, True)
                if at == 0:
                    ebuf[here, pl.ds(0, part)] = coeff.astype(jnp.bfloat16)
                    rows_acc[block_here, :] -= coeff
                else:
                    negative = (-coeff).astype(jnp.bfloat16)
                    if last:
                        elast[here, :] = negative
                    else:
                        ebuf[here, pl.ds(part, part)] = negative
                    rows_acc[block_here, :] += coeff
                if ahead:
                    other, _ = sums(dist(block_there, there, at), True, False)
                    total = total + fold(value - other if at == 0 else other - value)
            return total

        total = lax.fori_loop(0, rows // step_rows, body, jnp.zeros((8, part), jnp.float32))
        if ahead:
            loss_acc[offset] += total
        if not last:
            acc[block(0, rows), :] += jnp.dot(
                ebuf[pl.ds(0, rows), here_cols], cols, preferred_element_type=jnp.float32)

    for c in local:
        c.wait()
    for chunk in (0, 1):
        row_norms(p, chunk)
        pair_arrived(0, chunk)
        row_norms(sib, chunk)
    both = (0, 1)

    def by_side(order):
        for near in (0, 1):
            @pl.when(high if near == 0 else jnp.logical_not(high))
            def _():
                order(near, 1 - near, -1 if near == 0 else 1)

    def near_second(near, far, sign):
        work(2 * sign, both, 0)

    def near_second_other(near, far, sign):
        work(2 * sign, both, 1)

    def near_third(near, far, sign):
        take(near, REACH, *everything)
        work(REACH * sign, both)

    def rest(near, far, sign):
        work(-2 * sign, both)
        take(far, REACH, 0, 1)
        work(-REACH * sign, (0,))
        take(far, REACH, 2, 3)
        work(-REACH * sign, (1,))

    by_kind(edge_first, next_first, inner_first)
    work(0, both, 0)
    by_kind(edge_second, next_second, nothing)
    work(1, both, 0)
    work(-1, both, 0)
    by_kind(edge_third, next_third, inner_third)
    by_side(near_second)
    for chunk in (0, 1):
        pair_arrived(1, chunk)
        pair_copy(2, chunk).start()
        row_norms(zp, chunk)
    ones = jnp.ones((8, count), jnp.bfloat16)
    for chunk in (0, 1):
        pair_arrived(2, chunk)
        row_norms(diag, chunk)
    centre = jnp.dot(ones, bb[pl.ds(0, count), :], preferred_element_type=jnp.float32)[0:1, :] * (1.0 / count)
    work(0, both, 1)
    by_kind(edge_fourth, next_fourth, nothing)
    work(1, both, 1)
    by_kind(edge_fifth, nothing, nothing)
    work(-1, both, 1)
    by_kind(edge_sixth, nothing, nothing)
    by_side(near_second_other)
    by_side(near_third)
    by_side(rest)

    def loss_copy(rel):
        q = (sib, zp, diag)[rel]
        return remote(loss_acc.at[q], loss_in.at[rel], loss_send.at[rel], loss_recv.at[rel], dev(b, q))

    for rel in range(3):
        loss_copy(rel).start()

    tail = cbuf[jnp.where(high, 2 * REACH, 0), pl.ds(part, part), :]

    def gather_rows(q):
        here = quarter(q)
        products = acc[here, :] + jnp.dot(elast[here, :], tail, preferred_element_type=jnp.float32)
        return products, jnp.sum(rows_acc[here, :], axis=1, keepdims=True)

    def as_row(r):
        return jnp.transpose(jnp.broadcast_to(r, (part, 128)))[0:8, :]

    def sib_copy(which):
        q = (diag, sib)[which]
        return remote(acc.at[quarter(q)], got.at[which], fin_send.at[which], fin_recv.at[which], dev(b, sib))

    sib_row_copy = remote(r_out.at[0], r_in.at[0], fin_send.at[2], fin_recv.at[2], dev(b, sib))
    z_row_copy = remote(r_out.at[1], r_in.at[1], fin_send.at[3], fin_recv.at[3], dev(b, zp))
    z_copy = remote(z_out, z_in, fin_send.at[4], fin_recv.at[4], dev(b, zp))

    products, r = gather_rows(diag)
    acc[quarter(diag), :] = products + r * centre
    r_out[0] = as_row(r)
    sib_row_copy.start()
    sib_copy(0).start()
    products, r = gather_rows(zp)
    acc[quarter(zp), :] = products + r * centre
    r_out[1] = as_row(r)
    products, r = gather_rows(sib)
    acc[quarter(sib), :] = products + r * bb[quarter(sib), :].astype(jnp.float32)
    sib_copy(1).start()
    sib_row_copy.wait_recv()
    r_out[1] += r_in[0]
    z_row_copy.start()
    sib_copy(0).wait_recv()
    z_out[...] = (acc[quarter(zp), :] + got[0]).astype(jnp.bfloat16)
    z_copy.start()
    mine = bb[quarter(p), :].astype(jnp.float32)
    products, r = gather_rows(p)
    grad = products + r * mine
    for rel in range(3):
        loss_copy(rel).wait_recv()
    total = loss_acc[p] + loss_in[0] + loss_in[1] + loss_in[2]
    loss_out[...] = jnp.sum(jnp.sum(total, axis=1, keepdims=True), axis=0, keepdims=True) * (1.0 / count)
    sib_copy(1).wait_recv()
    z_row_copy.wait_recv()
    far = jnp.transpose(jnp.broadcast_to(r_in[1, 0:1, :], (128, part)))[:, 0:1]
    grad = grad + got[1] + far * (mine - centre)
    z_copy.wait_recv()
    grad_out[...] = grad + z_in[...].astype(jnp.float32)

    for chunk in range(CHUNKS):
        for way in (0, 1):
            for step in range(1, REACH + 1):
                if step == REACH and chunk in SIDE:
                    @pl.when(jnp.logical_not(is_top if way == 0 else is_bottom))
                    def _():
                        dp_copy(way, step, chunk).wait_send()
                else:
                    dp_copy(way, step, chunk).wait_send()
    for way in (0, 1):
        @pl.when(is_top if way == 0 else is_bottom)
        def _():
            for step in range(1, REACH + 1):
                for chunk in RELAYED if step < REACH else relayed_last:
                    pass_copy(way, step, chunk).wait_send()

        @pl.when(near_top if way == 0 else near_bottom)
        def _():
            for chunk in SIDE:
                side_copy(way, chunk).wait_send()
                side_pass_copy(way, chunk).wait_send()
    for chunk in (0, 1):
        for rel in range(3):
            pair_copy(rel, chunk).wait_send()
    for rel in range(3):
        loss_copy(rel).wait_send()
    sib_copy(0).wait_send()
    sib_copy(1).wait_send()
    sib_row_copy.wait_send()
    z_row_copy.wait_send()
    z_copy.wait_send()


def local_part(student, teacher, band_codes):
    part, width = student.shape
    count = 4 * part
    slots = 2 * REACH + 1
    piece = 2 * part // CHUNKS
    relayed = len(RELAYED)
    vmem = pl.BlockSpec(memory_space=pltpu.VMEM)
    anywhere = pl.BlockSpec(memory_space=pl.ANY)
    dma = pltpu.SemaphoreType.DMA
    return pl.pallas_call(
        kernel,
        out_shape=(
            jax.ShapeDtypeStruct((1, 1), jnp.float32),
            jax.ShapeDtypeStruct((part, width), jnp.float32),
        ),
        in_specs=[anywhere, anywhere, pl.BlockSpec(memory_space=pltpu.SMEM)],
        out_specs=(vmem, vmem),
        scratch_shapes=[
            pltpu.VMEM((2 * count, width), jnp.bfloat16),
            pltpu.VMEM((slots, 2 * part, width), jnp.bfloat16),
            pltpu.VMEM((REACH, relayed, piece, width), jnp.bfloat16),
            pltpu.VMEM((len(SIDE), piece, width), jnp.bfloat16),
            pltpu.VMEM((2 * count, 128), jnp.float32),
            pltpu.VMEM((slots, 8, 2 * part), jnp.float32),
            pltpu.VMEM((2 * count, 2 * part), jnp.float32),
            pltpu.VMEM((count, 2 * part), jnp.bfloat16),
            pltpu.VMEM((count, part), jnp.bfloat16),
            pltpu.VMEM((count, width), jnp.float32),
            pltpu.VMEM((count, part), jnp.float32),
            pltpu.VMEM((REACH + 1, 8, part), jnp.float32),
            pltpu.VMEM((3, 8, part), jnp.float32),
            pltpu.VMEM((2, part, width), jnp.float32),
            pltpu.VMEM((part, width), jnp.bfloat16),
            pltpu.VMEM((part, width), jnp.bfloat16),
            pltpu.VMEM((2, 8, 128), jnp.float32),
            pltpu.VMEM((2, 8, 128), jnp.float32),
            dma((2, 2)),
            dma((2, REACH, CHUNKS)),
            dma((2, REACH, CHUNKS)),
            dma((REACH, relayed)),
            dma((REACH, relayed)),
            dma((len(SIDE),)),
            dma((len(SIDE),)),
            dma((len(SIDE),)),
            dma((3, 2)),
            dma((3, 2)),
            dma((5,)),
            dma((5,)),
            dma((3,)),
            dma((3,)),
        ],
        compiler_params=pltpu.CompilerParams(
            collective_id=0, has_side_effects=True, vmem_limit_bytes=60 * 1024 * 1024
        ),
    )(student, teacher, band_codes)


def solution(mesh):
    return jax.shard_map(
        local_part,
        mesh=mesh,
        in_specs=(P(("dp", "pair"), None), P(("dp", "pair"), None), P()),
        out_specs=(P("dp", "pair"), P(("dp", "pair"), None)),
        check_vma=False,
    )
```

```python
import jax
import jax.numpy as jnp
from jax import lax
from jax.experimental import pallas as pl
from jax.experimental.pallas import tpu as pltpu
from jax.sharding import PartitionSpec as P

REACH = 3
ROW = 8
CHUNKS = 4
RELAYED = (1, 3)
SIDE = (0, 1)
LOG2E = 1.4426950408889634


def kernel(student, teacher, codes, loss_out, grad_out,
           bb, cbuf, hold, side_hold, nb, nc, inner, ebuf, elast, acc, rows_acc, loss_acc, loss_in,
           got, z_out, z_in, r_out, r_in,
           local_sem, dp_send, dp_recv, hold_send, hold_recv, side_send, side_recv, side_pass, pair_send, pair_recv,
           fin_send, fin_recv, loss_send, loss_recv):
    n_dp = lax.axis_size("dp")
    part, width = student.shape
    count = 4 * part
    piece = 2 * part // CHUNKS
    bands = codes.shape[0]
    b = lax.axis_index("dp")
    p = lax.axis_index("pair")
    z_lo = p // 2
    core = p % 2
    sib = z_lo * 2 + (1 - core)
    zp = (1 - z_lo) * 2 + core
    diag = (1 - z_lo) * 2 + (1 - core)
    up = (b + 1) % n_dp
    down = (b + n_dp - 1) % n_dp
    column = b % ROW
    is_top = column == ROW - 1
    is_bottom = column == 0
    up_row = (b + ROW) % n_dp
    down_row = (b + n_dp - ROW) % n_dp
    row_bottom = b - column
    row_top = row_bottom + ROW - 1

    def dev(block, place):
        return {"dp": block, "pair": place}

    def rows_of(q, chunk):
        return pl.ds(pl.multiple_of(chunk * count + q * part, part), part)

    def quarter(q):
        return pl.ds(pl.multiple_of(q * part, part), part)

    barrier = pltpu.get_barrier_semaphore()

    def greet(*targets):
        for target in targets:
            pl.semaphore_signal(barrier, inc=1, device_id=target, device_id_type=pl.DeviceIdType.MESH)

    greet(dev(up, p), dev(down, p), dev(b, sib), dev(b, zp), dev(b, diag))
    near_top = column == ROW - 2
    near_bottom = column == 1
    is_edge = jnp.logical_or(is_top, is_bottom)
    is_next = jnp.logical_or(near_top, near_bottom)

    @pl.when(is_top)
    def _():
        greet(dev(up_row, p), dev(down_row, p), dev(row_bottom, p), dev(row_bottom + 1, p))
        pl.semaphore_wait(barrier, 9)

    @pl.when(is_bottom)
    def _():
        greet(dev(up_row, p), dev(down_row, p), dev(row_top, p), dev(row_top - 1, p))
        pl.semaphore_wait(barrier, 9)

    @pl.when(near_top)
    def _():
        greet(dev(up_row, p), dev(down_row, p), dev(row_bottom, p))
        pl.semaphore_wait(barrier, 8)

    @pl.when(near_bottom)
    def _():
        greet(dev(up_row, p), dev(down_row, p), dev(row_top, p))
        pl.semaphore_wait(barrier, 8)

    @pl.when(jnp.logical_not(jnp.logical_or(is_edge, is_next)))
    def _():
        pl.semaphore_wait(barrier, 5)

    own = (student, teacher)

    def remote(src, dst, ssem, rsem, target):
        return pltpu.make_async_remote_copy(
            src_ref=src, dst_ref=dst, send_sem=ssem, recv_sem=rsem,
            device_id=target, device_id_type=pl.DeviceIdType.MESH)

    def own_piece(chunk):
        first = chunk * piece
        return own[first // part].at[pl.ds(first % part, piece)]

    def slot_piece(slot, chunk):
        return cbuf.at[slot, pl.ds(chunk * piece, piece)]

    def dp_copy(way, step, chunk):
        sign = -1 if way == 0 else 1
        src = own_piece(chunk) if step == 1 else slot_piece(REACH + sign * (step - 1), chunk)
        return remote(src, slot_piece(REACH + sign * step, chunk),
                      dp_send.at[way, step - 1, chunk], dp_recv.at[way, step - 1, chunk],
                      dev(up if way == 0 else down, p))

    def hold_copy(way, step, chunk):
        sign = -1 if way == 0 else 1
        src = own_piece(chunk) if step == 1 else slot_piece(REACH + sign * (step - 1), chunk)
        index = RELAYED.index(chunk)
        return remote(src, hold.at[step - 1, index], dp_send.at[way, step - 1, chunk],
                      hold_recv.at[step - 1, index], dev(up_row if way == 0 else down_row, p))

    def pass_copy(way, step, chunk):
        sign = -1 if way == 0 else 1
        index = RELAYED.index(chunk)
        return remote(hold.at[step - 1, index], slot_piece(REACH + sign * step, chunk),
                      hold_send.at[step - 1, index], dp_recv.at[way, step - 1, chunk],
                      dev(row_bottom if way == 0 else row_top, p))

    def side_copy(way, chunk):
        sign = -1 if way == 0 else 1
        index = SIDE.index(chunk)
        return remote(slot_piece(REACH + sign, chunk), side_hold.at[index], side_send.at[index], side_recv.at[index],
                      dev(up_row if way == 0 else down_row, p))

    def side_pass_copy(way, chunk):
        sign = -1 if way == 0 else 1
        index = SIDE.index(chunk)
        return remote(side_hold.at[index], slot_piece(REACH + sign * REACH, chunk), side_pass.at[index],
                      dp_recv.at[way, REACH - 1, chunk], dev(row_bottom if way == 0 else row_top, p))

    def dp_start(way, step, chunk):
        edge = is_top if way == 0 else is_bottom
        by_side = step == REACH and chunk in SIDE
        if by_side or chunk in RELAYED:
            if not by_side:
                @pl.when(edge)
                def _():
                    hold_copy(way, step, chunk).start()

            @pl.when(jnp.logical_not(edge))
            def _():
                dp_copy(way, step, chunk).start()
        else:
            dp_copy(way, step, chunk).start()

    def relay(way, step, *chunks):
        for chunk in chunks:
            hold_copy(way, step, chunk).wait_recv()
            pass_copy(way, step, chunk).start()

    def side_relay(way):
        for chunk in SIDE:
            side_copy(way, chunk).wait_recv()
            side_pass_copy(way, chunk).start()

    def take(way, step, *chunks):
        for chunk in chunks:
            dp_copy(way, step, chunk).wait_recv()
            if step < REACH:
                dp_start(way, step + 1, chunk)

    high = column >= ROW // 2
    everything = tuple(range(CHUNKS))
    straight = tuple(c for c in everything if c not in RELAYED)
    relayed_last = tuple(c for c in RELAYED if c not in SIDE)

    def by_kind(edge_order, next_order, inner_order):
        for near in (0, 1):
            far = 1 - near
            for chosen, order in ((is_edge, edge_order), (is_next, next_order),
                                  (jnp.logical_not(jnp.logical_or(is_edge, is_next)), inner_order)):
                @pl.when(jnp.logical_and(chosen, high if near == 0 else jnp.logical_not(high)))
                def _():
                    order(near, far)

    def edge_first(near, far):
        take(near, 1, 0, 1)
        relay(near, 1, RELAYED[0])
        take(near, 1, 2, 3)
        relay(near, 1, RELAYED[1])
        take(far, 1, *straight)

    def next_first(near, far):
        for chunk in everything:
            take(near, 1, chunk)
            take(far, 1, chunk)
        for chunk in SIDE:
            side_copy(near, chunk).start()

    def inner_first(near, far):
        for chunk in everything:
            take(near, 1, chunk)
            take(far, 1, chunk)

    def edge_second(near, far):
        take(far, 1, *RELAYED)

    def next_second(near, far):
        side_relay(near)

    def nothing(near, far):
        pass

    def edge_third(near, far):
        take(near, 2, 0, 1)
        relay(near, 2, RELAYED[0])
        take(near, 2, 2, 3)
        relay(near, 2, RELAYED[1])

    def next_third(near, far):
        take(near, 2, *everything)

    def inner_third(near, far):
        for chunk in everything:
            take(near, 2, chunk)
            take(far, 2, chunk)

    def edge_fourth(near, far):
        take(far, 2, *straight)

    def edge_fifth(near, far):
        take(far, 2, *RELAYED)

    def edge_sixth(near, far):
        relay(near, 3, *relayed_last)

    def next_fourth(near, far):
        take(far, 2, *everything)

    def pair_copy(rel, chunk):
        if rel == 2:
            src = dst = bb.at[rows_of(zp, chunk)]
        else:
            src, dst = own[chunk], bb.at[rows_of(p, chunk)]
        target = dev(b, zp if rel == 1 else sib)
        return remote(src, dst, pair_send.at[rel, chunk], pair_recv.at[rel, chunk], target)

    def pair_arrived(rel, chunk):
        q = (sib, zp, diag)[rel]
        ref = bb.at[rows_of(q, chunk)]
        remote(ref, ref, pair_send.at[rel, chunk], pair_recv.at[rel, chunk], dev(b, sib)).wait_recv()

    local = [pltpu.make_async_copy(own[c], cbuf.at[REACH, pl.ds(c * part, part)], local_sem.at[0, c]) for c in (0, 1)]
    local += [pltpu.make_async_copy(own[c], bb.at[rows_of(p, c)], local_sem.at[1, c]) for c in (0, 1)]
    for chunk in range(CHUNKS):
        for way in (0, 1):
            dp_start(way, 1, chunk)
        if chunk == 1:
            pair_copy(1, 0).start()
            pair_copy(0, 0).start()
    pair_copy(0, 1).start()
    for c in local:
        c.start()

    scale = [2.0 / (codes[m].astype(jnp.float32) * width) for m in range(bands)]
    expo = [s * (-LOG2E) for s in scale]
    factor = 2.0 * width / count
    slope = [s * factor for s in scale]

    acc[...] = jnp.zeros_like(acc)
    rows_acc[...] = jnp.zeros_like(rows_acc)
    loss_acc[...] = jnp.zeros_like(loss_acc)

    def split_squares(x):
        sq = jnp.square(x.astype(jnp.float32))
        hi = sq.astype(jnp.bfloat16)
        lo = (sq - hi.astype(jnp.float32)).astype(jnp.bfloat16)
        return hi, lo

    def nt(x, y):
        return lax.dot_general(x, y, (((1,), (1,)), ((), ())), preferred_element_type=jnp.float32)

    def row_norms(q, chunk):
        here = rows_of(q, chunk)
        hi, lo = split_squares(bb[here, :])
        ones = jnp.ones((128, width), jnp.bfloat16)
        nb[here, :] = nt(hi, ones) + nt(lo, ones)

    step_rows = 128

    def col_norms(offset, parts):
        slot = REACH + offset
        here = pl.ds(parts[0] * part, len(parts) * part)
        sq = jnp.square(cbuf[slot, here, :].astype(jnp.float32))
        folded = sq[:, 0:128]
        for k in range(1, width // 128):
            folded = folded + sq[:, k * 128:(k + 1) * 128]
        norms = jnp.sum(jnp.transpose(folded), axis=0, keepdims=True)
        nc[slot, :, here] = jnp.broadcast_to(norms, (8, len(parts) * part))

    chip_rows = 2 * part

    def work(offset, parts, chip=None):
        slot = REACH + offset
        ahead = offset >= 0
        last = abs(offset) == REACH and parts == (1,)
        weight = [2.0 * w for w in slope] if offset == 0 else slope
        here_cols = pl.ds(parts[0] * part, len(parts) * part)
        if chip is None:
            base, rows = 0, count
        else:
            base, rows = (z_lo if chip == 0 else 1 - z_lo) * chip_rows, chip_rows
        if chip != 1:
            col_norms(offset, parts)
        cols = cbuf[slot, here_cols, :]

        def block(first, size):
            return pl.ds(pl.multiple_of(base + first, size), size)

        inner[pl.ds(0, rows), here_cols] = nt(bb[block(0, rows), :], cols)
        if offset == 0:
            teacher_cols = pl.ds(part, part)
            inner[pl.ds(count, rows), teacher_cols] = nt(bb[block(count, rows), :], cols[part:, :])
        elif ahead:
            inner[pl.ds(count, rows), here_cols] = nt(bb[block(count, rows), :], cols)

        def dist(norm_rows, here, at):
            norm = nb[norm_rows, :] + nc[slot, 0:1, pl.ds(at * part, part)]
            return norm - 2.0 * inner[here, pl.ds(at * part, part)]

        def sums(d, want_value, want_slope):
            value = slope_sum = None
            for m in range(bands):
                term = jnp.exp2(d * expo[m])
                if want_value:
                    value = term if value is None else value + term
                if want_slope:
                    scaled = term * weight[m]
                    slope_sum = scaled if slope_sum is None else slope_sum + scaled
            return value, slope_sum

        def fold(x):
            return jnp.sum(x.reshape(step_rows // 8, 8, part), axis=0)

        def body(i, total):
            here = pl.ds(pl.multiple_of(i * step_rows, step_rows), step_rows)
            there = pl.ds(pl.multiple_of(count + i * step_rows, step_rows), step_rows)
            block_here = block(i * step_rows, step_rows)
            block_there = block(count + i * step_rows, step_rows)
            for at in parts:
                value, coeff = sums(dist(block_here, here, at), ahead, True)
                if at == 0:
                    ebuf[here, pl.ds(0, part)] = coeff.astype(jnp.bfloat16)
                    rows_acc[block_here, :] -= coeff
                else:
                    negative = (-coeff).astype(jnp.bfloat16)
                    if last:
                        elast[here, :] = negative
                    else:
                        ebuf[here, pl.ds(part, part)] = negative
                    rows_acc[block_here, :] += coeff
                if offset == 0 and at == 0:
                    total = total + fold(value)
                elif ahead:
                    other, _ = sums(dist(block_there, there, at), True, False)
                    if offset == 0:
                        value = 2.0 * value
                    total = total + fold(value - other if at == 0 else other - value)
            return total

        total = lax.fori_loop(0, rows // step_rows, body, jnp.zeros((8, part), jnp.float32))
        if ahead:
            loss_acc[offset] += total
        if not last:
            acc[block(0, rows), :] += jnp.dot(
                ebuf[pl.ds(0, rows), here_cols], cols, preferred_element_type=jnp.float32)

    for c in local:
        c.wait()
    for chunk in (0, 1):
        row_norms(p, chunk)
        pair_arrived(0, chunk)
        row_norms(sib, chunk)
    both = (0, 1)

    def by_side(order):
        for near in (0, 1):
            @pl.when(high if near == 0 else jnp.logical_not(high))
            def _():
                order(near, 1 - near, -1 if near == 0 else 1)

    def near_second(near, far, sign):
        work(2 * sign, both, 0)

    def near_second_other(near, far, sign):
        work(2 * sign, both, 1)

    def near_third(near, far, sign):
        take(near, REACH, *everything)
        work(REACH * sign, both)

    def far_second(near, far, sign):
        work(-2 * sign, both)

    def rest(near, far, sign):
        take(far, REACH, 0, 1)
        work(-REACH * sign, (0,))
        take(far, REACH, 2, 3)
        work(-REACH * sign, (1,))

    by_kind(edge_first, next_first, inner_first)
    pair_copy(1, 1).start()
    work(0, both, 0)
    by_kind(edge_second, next_second, nothing)
    work(1, both, 0)
    work(-1, both, 0)
    by_kind(edge_third, next_third, inner_third)
    by_side(near_second)
    for chunk in (0, 1):
        pair_arrived(1, chunk)
        pair_copy(2, chunk).start()
        row_norms(zp, chunk)
    ones = jnp.ones((8, count), jnp.bfloat16)
    for chunk in (0, 1):
        pair_arrived(2, chunk)
        row_norms(diag, chunk)
    centre = jnp.dot(ones, bb[pl.ds(0, count), :], preferred_element_type=jnp.float32)[0:1, :] * (1.0 / count)
    by_kind(edge_fourth, next_fourth, nothing)
    work(0, both, 1)
    work(1, both, 1)
    by_kind(edge_fifth, nothing, nothing)
    work(-1, both, 1)
    by_kind(edge_sixth, nothing, nothing)
    by_side(near_second_other)
    by_side(near_third)
    by_side(far_second)
    by_side(rest)

    def loss_copy(rel):
        q = (sib, zp, diag)[rel]
        return remote(loss_acc.at[q], loss_in.at[rel], loss_send.at[rel], loss_recv.at[rel], dev(b, q))

    for rel in range(3):
        loss_copy(rel).start()

    tail = cbuf[jnp.where(high, 2 * REACH, 0), pl.ds(part, part), :]

    def gather_rows(q):
        here = quarter(q)
        products = acc[here, :] + jnp.dot(elast[here, :], tail, preferred_element_type=jnp.float32)
        return products, jnp.sum(rows_acc[here, :], axis=1, keepdims=True)

    def as_row(r):
        return jnp.transpose(jnp.broadcast_to(r, (part, 128)))[0:8, :]

    def sib_copy(which):
        q = (diag, sib)[which]
        return remote(acc.at[quarter(q)], got.at[which], fin_send.at[which], fin_recv.at[which], dev(b, sib))

    sib_row_copy = remote(r_out.at[0], r_in.at[0], fin_send.at[2], fin_recv.at[2], dev(b, sib))
    z_row_copy = remote(r_out.at[1], r_in.at[1], fin_send.at[3], fin_recv.at[3], dev(b, zp))
    z_copy = remote(z_out, z_in, fin_send.at[4], fin_recv.at[4], dev(b, zp))

    products, r = gather_rows(diag)
    acc[quarter(diag), :] = products + r * centre
    r_out[0] = as_row(r)
    sib_row_copy.start()
    sib_copy(0).start()
    products, r = gather_rows(zp)
    acc[quarter(zp), :] = products + r * centre
    r_out[1] = as_row(r)
    products, r = gather_rows(sib)
    acc[quarter(sib), :] = products + r * bb[quarter(sib), :].astype(jnp.float32)
    sib_copy(1).start()
    sib_row_copy.wait_recv()
    r_out[1] += r_in[0]
    z_row_copy.start()
    sib_copy(0).wait_recv()
    z_out[...] = (acc[quarter(zp), :] + got[0]).astype(jnp.bfloat16)
    z_copy.start()
    mine = bb[quarter(p), :].astype(jnp.float32)
    products, r = gather_rows(p)
    grad = products + r * mine
    for rel in range(3):
        loss_copy(rel).wait_recv()
    total = loss_acc[p] + loss_in[0] + loss_in[1] + loss_in[2]
    loss_out[...] = jnp.sum(jnp.sum(total, axis=1, keepdims=True), axis=0, keepdims=True) * (1.0 / count)
    sib_copy(1).wait_recv()
    z_row_copy.wait_recv()
    far = jnp.transpose(jnp.broadcast_to(r_in[1, 0:1, :], (128, part)))[:, 0:1]
    grad = grad + got[1] + far * (mine - centre)
    z_copy.wait_recv()
    grad_out[...] = grad + z_in[...].astype(jnp.float32)

    for chunk in range(CHUNKS):
        for way in (0, 1):
            for step in range(1, REACH + 1):
                if step == REACH and chunk in SIDE:
                    @pl.when(jnp.logical_not(is_top if way == 0 else is_bottom))
                    def _():
                        dp_copy(way, step, chunk).wait_send()
                else:
                    dp_copy(way, step, chunk).wait_send()
    for way in (0, 1):
        @pl.when(is_top if way == 0 else is_bottom)
        def _():
            for step in range(1, REACH + 1):
                for chunk in RELAYED if step < REACH else relayed_last:
                    pass_copy(way, step, chunk).wait_send()

        @pl.when(near_top if way == 0 else near_bottom)
        def _():
            for chunk in SIDE:
                side_copy(way, chunk).wait_send()
                side_pass_copy(way, chunk).wait_send()
    for chunk in (0, 1):
        for rel in range(3):
            pair_copy(rel, chunk).wait_send()
    for rel in range(3):
        loss_copy(rel).wait_send()
    sib_copy(0).wait_send()
    sib_copy(1).wait_send()
    sib_row_copy.wait_send()
    z_row_copy.wait_send()
    z_copy.wait_send()


def local_part(student, teacher, band_codes):
    part, width = student.shape
    count = 4 * part
    slots = 2 * REACH + 1
    piece = 2 * part // CHUNKS
    relayed = len(RELAYED)
    vmem = pl.BlockSpec(memory_space=pltpu.VMEM)
    anywhere = pl.BlockSpec(memory_space=pl.ANY)
    dma = pltpu.SemaphoreType.DMA
    return pl.pallas_call(
        kernel,
        out_shape=(
            jax.ShapeDtypeStruct((1, 1), jnp.float32),
            jax.ShapeDtypeStruct((part, width), jnp.float32),
        ),
        in_specs=[anywhere, anywhere, pl.BlockSpec(memory_space=pltpu.SMEM)],
        out_specs=(vmem, vmem),
        scratch_shapes=[
            pltpu.VMEM((2 * count, width), jnp.bfloat16),
            pltpu.VMEM((slots, 2 * part, width), jnp.bfloat16),
            pltpu.VMEM((REACH, relayed, piece, width), jnp.bfloat16),
            pltpu.VMEM((len(SIDE), piece, width), jnp.bfloat16),
            pltpu.VMEM((2 * count, 128), jnp.float32),
            pltpu.VMEM((slots, 8, 2 * part), jnp.float32),
            pltpu.VMEM((2 * count, 2 * part), jnp.float32),
            pltpu.VMEM((count, 2 * part), jnp.bfloat16),
            pltpu.VMEM((count, part), jnp.bfloat16),
            pltpu.VMEM((count, width), jnp.float32),
            pltpu.VMEM((count, part), jnp.float32),
            pltpu.VMEM((REACH + 1, 8, part), jnp.float32),
            pltpu.VMEM((3, 8, part), jnp.float32),
            pltpu.VMEM((2, part, width), jnp.float32),
            pltpu.VMEM((part, width), jnp.bfloat16),
            pltpu.VMEM((part, width), jnp.bfloat16),
            pltpu.VMEM((2, 8, 128), jnp.float32),
            pltpu.VMEM((2, 8, 128), jnp.float32),
            dma((2, 2)),
            dma((2, REACH, CHUNKS)),
            dma((2, REACH, CHUNKS)),
            dma((REACH, relayed)),
            dma((REACH, relayed)),
            dma((len(SIDE),)),
            dma((len(SIDE),)),
            dma((len(SIDE),)),
            dma((3, 2)),
            dma((3, 2)),
            dma((5,)),
            dma((5,)),
            dma((3,)),
            dma((3,)),
        ],
        compiler_params=pltpu.CompilerParams(
            collective_id=0, has_side_effects=True, vmem_limit_bytes=60 * 1024 * 1024
        ),
    )(student, teacher, band_codes)


def solution(mesh):
    return jax.shard_map(
        local_part,
        mesh=mesh,
        in_specs=(P(("dp", "pair"), None), P(("dp", "pair"), None), P()),
        out_specs=(P("dp", "pair"), P(("dp", "pair"), None)),
        check_vma=False,
    )
```

```python
import jax
import jax.numpy as jnp
from jax import lax
from jax.experimental import pallas as pl
from jax.experimental.pallas import tpu as pltpu
from jax.sharding import PartitionSpec as P

REACH = 3
ROW = 8
CHUNKS = 4
RELAYED = (1, 3)
SIDE = (0, 1)
LOG2E = 1.4426950408889634


def kernel(student, teacher, codes, loss_out, grad_out, far_out,
           bb, cbuf, hold, side_hold, nb, nc, inner, ebuf, elast, acc, rows_acc, loss_acc, loss_in,
           got, z_out, z_in, r_out, r_in,
           local_sem, dp_send, dp_recv, hold_send, hold_recv, side_send, side_recv, side_pass, pair_send, pair_recv,
           fin_send, fin_recv, loss_send, loss_recv):
    n_dp = lax.axis_size("dp")
    part, width = student.shape
    count = 4 * part
    piece = 2 * part // CHUNKS
    bands = codes.shape[0]
    b = lax.axis_index("dp")
    p = lax.axis_index("pair")
    z_lo = p // 2
    core = p % 2
    sib = z_lo * 2 + (1 - core)
    zp = (1 - z_lo) * 2 + core
    diag = (1 - z_lo) * 2 + (1 - core)
    up = (b + 1) % n_dp
    down = (b + n_dp - 1) % n_dp
    column = b % ROW
    is_top = column == ROW - 1
    is_bottom = column == 0
    up_row = (b + ROW) % n_dp
    down_row = (b + n_dp - ROW) % n_dp
    row_bottom = b - column
    row_top = row_bottom + ROW - 1

    def dev(block, place):
        return {"dp": block, "pair": place}

    def rows_of(q, chunk):
        return pl.ds(pl.multiple_of(chunk * count + q * part, part), part)

    def quarter(q):
        return pl.ds(pl.multiple_of(q * part, part), part)

    barrier = pltpu.get_barrier_semaphore()

    def greet(*targets):
        for target in targets:
            pl.semaphore_signal(barrier, inc=1, device_id=target, device_id_type=pl.DeviceIdType.MESH)

    greet(dev(up, p), dev(down, p), dev(b, sib), dev(b, zp), dev(b, diag))
    near_top = column == ROW - 2
    near_bottom = column == 1
    is_edge = jnp.logical_or(is_top, is_bottom)
    is_next = jnp.logical_or(near_top, near_bottom)

    @pl.when(is_top)
    def _():
        greet(dev(up_row, p), dev(down_row, p), dev(row_bottom, p), dev(row_bottom + 1, p))
        pl.semaphore_wait(barrier, 9)

    @pl.when(is_bottom)
    def _():
        greet(dev(up_row, p), dev(down_row, p), dev(row_top, p), dev(row_top - 1, p))
        pl.semaphore_wait(barrier, 9)

    @pl.when(near_top)
    def _():
        greet(dev(up_row, p), dev(down_row, p), dev(row_bottom, p))
        pl.semaphore_wait(barrier, 8)

    @pl.when(near_bottom)
    def _():
        greet(dev(up_row, p), dev(down_row, p), dev(row_top, p))
        pl.semaphore_wait(barrier, 8)

    @pl.when(jnp.logical_not(jnp.logical_or(is_edge, is_next)))
    def _():
        pl.semaphore_wait(barrier, 5)

    own = (student, teacher)

    def remote(src, dst, ssem, rsem, target):
        return pltpu.make_async_remote_copy(
            src_ref=src, dst_ref=dst, send_sem=ssem, recv_sem=rsem,
            device_id=target, device_id_type=pl.DeviceIdType.MESH)

    def own_piece(chunk):
        first = chunk * piece
        return own[first // part].at[pl.ds(first % part, piece)]

    def slot_piece(slot, chunk):
        return cbuf.at[slot, pl.ds(chunk * piece, piece)]

    def dp_copy(way, step, chunk):
        sign = -1 if way == 0 else 1
        src = own_piece(chunk) if step == 1 else slot_piece(REACH + sign * (step - 1), chunk)
        return remote(src, slot_piece(REACH + sign * step, chunk),
                      dp_send.at[way, step - 1, chunk], dp_recv.at[way, step - 1, chunk],
                      dev(up if way == 0 else down, p))

    def hold_copy(way, step, chunk):
        sign = -1 if way == 0 else 1
        src = own_piece(chunk) if step == 1 else slot_piece(REACH + sign * (step - 1), chunk)
        index = RELAYED.index(chunk)
        return remote(src, hold.at[step - 1, index], dp_send.at[way, step - 1, chunk],
                      hold_recv.at[step - 1, index], dev(up_row if way == 0 else down_row, p))

    def pass_copy(way, step, chunk):
        sign = -1 if way == 0 else 1
        index = RELAYED.index(chunk)
        return remote(hold.at[step - 1, index], slot_piece(REACH + sign * step, chunk),
                      hold_send.at[step - 1, index], dp_recv.at[way, step - 1, chunk],
                      dev(row_bottom if way == 0 else row_top, p))

    def side_copy(way, chunk):
        sign = -1 if way == 0 else 1
        index = SIDE.index(chunk)
        return remote(slot_piece(REACH + sign, chunk), side_hold.at[index], side_send.at[index], side_recv.at[index],
                      dev(up_row if way == 0 else down_row, p))

    def side_pass_copy(way, chunk):
        sign = -1 if way == 0 else 1
        index = SIDE.index(chunk)
        return remote(side_hold.at[index], slot_piece(REACH + sign * REACH, chunk), side_pass.at[index],
                      dp_recv.at[way, REACH - 1, chunk], dev(row_bottom if way == 0 else row_top, p))

    def dp_start(way, step, chunk):
        edge = is_top if way == 0 else is_bottom
        by_side = step == REACH and chunk in SIDE
        if by_side or chunk in RELAYED:
            if not by_side:
                @pl.when(edge)
                def _():
                    hold_copy(way, step, chunk).start()

            @pl.when(jnp.logical_not(edge))
            def _():
                dp_copy(way, step, chunk).start()
        else:
            dp_copy(way, step, chunk).start()

    def relay(way, step, *chunks):
        for chunk in chunks:
            hold_copy(way, step, chunk).wait_recv()
            pass_copy(way, step, chunk).start()

    def side_relay(way):
        for chunk in SIDE:
            side_copy(way, chunk).wait_recv()
            side_pass_copy(way, chunk).start()

    def take(way, step, *chunks):
        for chunk in chunks:
            dp_copy(way, step, chunk).wait_recv()
            if step < REACH:
                dp_start(way, step + 1, chunk)

    high = column >= ROW // 2
    everything = tuple(range(CHUNKS))
    straight = tuple(c for c in everything if c not in RELAYED)
    relayed_last = tuple(c for c in RELAYED if c not in SIDE)

    def by_kind(edge_order, next_order, inner_order):
        for near in (0, 1):
            far = 1 - near
            for chosen, order in ((is_edge, edge_order), (is_next, next_order),
                                  (jnp.logical_not(jnp.logical_or(is_edge, is_next)), inner_order)):
                @pl.when(jnp.logical_and(chosen, high if near == 0 else jnp.logical_not(high)))
                def _():
                    order(near, far)

    def edge_first(near, far):
        take(near, 1, 0, 1)
        relay(near, 1, RELAYED[0])
        take(near, 1, 2, 3)
        relay(near, 1, RELAYED[1])

    def next_first(near, far):
        for chunk in everything:
            take(near, 1, chunk)
            take(far, 1, chunk)
        for chunk in SIDE:
            side_copy(near, chunk).start()

    def inner_first(near, far):
        for chunk in everything:
            take(near, 1, chunk)
            take(far, 1, chunk)

    def edge_second(near, far):
        take(far, 1, *straight)
        take(far, 1, *RELAYED)

    def next_second(near, far):
        side_relay(near)

    def nothing(near, far):
        pass

    def edge_third(near, far):
        take(near, 2, 0, 1)
        relay(near, 2, RELAYED[0])
        take(near, 2, 2, 3)
        relay(near, 2, RELAYED[1])

    def next_third(near, far):
        take(near, 2, *everything)

    def inner_third(near, far):
        for chunk in everything:
            take(near, 2, chunk)
            take(far, 2, chunk)

    def edge_fourth(near, far):
        take(far, 2, *straight)

    def edge_fifth(near, far):
        take(far, 2, *RELAYED)

    def edge_sixth(near, far):
        relay(near, 3, *relayed_last)

    def next_fourth(near, far):
        take(far, 2, *everything)

    def pair_copy(rel, chunk):
        if rel == 2:
            src = dst = bb.at[rows_of(zp, chunk)]
        else:
            src, dst = own[chunk], bb.at[rows_of(p, chunk)]
        target = dev(b, zp if rel == 1 else sib)
        return remote(src, dst, pair_send.at[rel, chunk], pair_recv.at[rel, chunk], target)

    def pair_arrived(rel, chunk):
        q = (sib, zp, diag)[rel]
        ref = bb.at[rows_of(q, chunk)]
        remote(ref, ref, pair_send.at[rel, chunk], pair_recv.at[rel, chunk], dev(b, sib)).wait_recv()

    local = [pltpu.make_async_copy(own[c], cbuf.at[REACH, pl.ds(c * part, part)], local_sem.at[0, c]) for c in (0, 1)]
    local += [pltpu.make_async_copy(own[c], bb.at[rows_of(p, c)], local_sem.at[1, c]) for c in (0, 1)]
    for chunk in range(CHUNKS):
        for way in (0, 1):
            dp_start(way, 1, chunk)
        if chunk == 1:
            pair_copy(1, 0).start()
            pair_copy(0, 0).start()
    pair_copy(0, 1).start()
    for c in local:
        c.start()

    scale = [2.0 / (codes[m].astype(jnp.float32) * width) for m in range(bands)]
    expo = [s * (-LOG2E) for s in scale]
    factor = 2.0 * width / count
    slope = [s * factor for s in scale]

    acc[...] = jnp.zeros_like(acc)
    rows_acc[...] = jnp.zeros_like(rows_acc)
    loss_acc[...] = jnp.zeros_like(loss_acc)

    def split_squares(x):
        sq = jnp.square(x.astype(jnp.float32))
        hi = sq.astype(jnp.bfloat16)
        lo = (sq - hi.astype(jnp.float32)).astype(jnp.bfloat16)
        return hi, lo

    def nt(x, y):
        return lax.dot_general(x, y, (((1,), (1,)), ((), ())), preferred_element_type=jnp.float32)

    def row_norms(q, chunk):
        here = rows_of(q, chunk)
        hi, lo = split_squares(bb[here, :])
        ones = jnp.ones((128, width), jnp.bfloat16)
        nb[here, :] = nt(hi, ones) + nt(lo, ones)

    step_rows = 128

    def col_norms(offset, parts):
        slot = REACH + offset
        here = pl.ds(parts[0] * part, len(parts) * part)
        sq = jnp.square(cbuf[slot, here, :].astype(jnp.float32))
        folded = sq[:, 0:128]
        for k in range(1, width // 128):
            folded = folded + sq[:, k * 128:(k + 1) * 128]
        norms = jnp.sum(jnp.transpose(folded), axis=0, keepdims=True)
        nc[slot, :, here] = jnp.broadcast_to(norms, (8, len(parts) * part))

    chip_rows = 2 * part

    def work(offset, parts, chip=None):
        slot = REACH + offset
        ahead = offset >= 0
        last = abs(offset) == REACH and parts == (1,)
        weight = [2.0 * w for w in slope] if offset == 0 else slope
        here_cols = pl.ds(parts[0] * part, len(parts) * part)
        if chip is None:
            base, rows = 0, count
        else:
            base, rows = (z_lo if chip == 0 else 1 - z_lo) * chip_rows, chip_rows
        if chip != 1:
            col_norms(offset, parts)
        cols = cbuf[slot, here_cols, :]

        def block(first, size):
            return pl.ds(pl.multiple_of(base + first, size), size)

        inner[pl.ds(0, rows), here_cols] = nt(bb[block(0, rows), :], cols)
        if offset == 0:
            teacher_cols = pl.ds(part, part)
            inner[pl.ds(count, rows), teacher_cols] = nt(bb[block(count, rows), :], cols[part:, :])
        elif ahead:
            inner[pl.ds(count, rows), here_cols] = nt(bb[block(count, rows), :], cols)

        def dist(norm_rows, here, at):
            norm = nb[norm_rows, :] + nc[slot, 0:1, pl.ds(at * part, part)]
            return norm - 2.0 * inner[here, pl.ds(at * part, part)]

        def sums(d, want_value, want_slope):
            value = slope_sum = None
            for m in range(bands):
                term = jnp.exp2(d * expo[m])
                if want_value:
                    value = term if value is None else value + term
                if want_slope:
                    scaled = term * weight[m]
                    slope_sum = scaled if slope_sum is None else slope_sum + scaled
            return value, slope_sum

        def fold(x):
            return jnp.sum(x.reshape(step_rows // 8, 8, part), axis=0)

        def body(i, total):
            here = pl.ds(pl.multiple_of(i * step_rows, step_rows), step_rows)
            there = pl.ds(pl.multiple_of(count + i * step_rows, step_rows), step_rows)
            block_here = block(i * step_rows, step_rows)
            block_there = block(count + i * step_rows, step_rows)
            for at in parts:
                value, coeff = sums(dist(block_here, here, at), ahead, True)
                if at == 0:
                    ebuf[here, pl.ds(0, part)] = coeff.astype(jnp.bfloat16)
                    rows_acc[block_here, :] -= coeff
                else:
                    negative = (-coeff).astype(jnp.bfloat16)
                    if last:
                        elast[here, :] = negative
                    else:
                        ebuf[here, pl.ds(part, part)] = negative
                    rows_acc[block_here, :] += coeff
                if offset == 0 and at == 0:
                    total = total + fold(value)
                elif ahead:
                    other, _ = sums(dist(block_there, there, at), True, False)
                    if offset == 0:
                        value = 2.0 * value
                    total = total + fold(value - other if at == 0 else other - value)
            return total

        total = lax.fori_loop(0, rows // step_rows, body, jnp.zeros((8, part), jnp.float32))
        if ahead:
            loss_acc[offset] += total
        if not last:
            acc[block(0, rows), :] += jnp.dot(
                ebuf[pl.ds(0, rows), here_cols], cols, preferred_element_type=jnp.float32)

    for c in local:
        c.wait()
    for chunk in (0, 1):
        row_norms(p, chunk)
        pair_arrived(0, chunk)
        row_norms(sib, chunk)
    both = (0, 1)

    def by_side(order):
        for near in (0, 1):
            @pl.when(high if near == 0 else jnp.logical_not(high))
            def _():
                order(near, 1 - near, -1 if near == 0 else 1)

    def near_second(near, far, sign):
        work(2 * sign, both, 0)

    def near_second_other(near, far, sign):
        work(2 * sign, both, 1)

    def near_third(near, far, sign):
        take(near, REACH, *everything)
        work(REACH * sign, both)

    def far_second(near, far, sign):
        work(-2 * sign, both)

    def rest(near, far, sign):
        take(far, REACH, 0, 1)
        work(-REACH * sign, (0,))
        take(far, REACH, 2, 3)
        work(-REACH * sign, (1,))

    by_kind(edge_first, next_first, inner_first)
    pair_copy(1, 1).start()
    work(0, both, 0)
    by_kind(edge_second, next_second, nothing)
    work(1, both, 0)
    work(-1, both, 0)
    by_kind(edge_third, next_third, inner_third)
    by_side(near_second)
    for chunk in (0, 1):
        pair_arrived(1, chunk)
        pair_copy(2, chunk).start()
        row_norms(zp, chunk)
    ones = jnp.ones((8, count), jnp.bfloat16)
    for chunk in (0, 1):
        pair_arrived(2, chunk)
        row_norms(diag, chunk)
    centre = jnp.dot(ones, bb[pl.ds(0, count), :], preferred_element_type=jnp.float32)[0:1, :] * (1.0 / count)
    by_kind(edge_fourth, next_fourth, nothing)
    work(0, both, 1)
    work(1, both, 1)
    by_kind(edge_fifth, nothing, nothing)
    work(-1, both, 1)
    by_kind(edge_sixth, nothing, nothing)
    by_side(near_second_other)
    by_side(near_third)
    by_side(far_second)
    by_side(rest)

    def loss_copy(rel):
        q = (sib, zp, diag)[rel]
        return remote(loss_acc.at[q], loss_in.at[rel], loss_send.at[rel], loss_recv.at[rel], dev(b, q))

    for rel in range(3):
        loss_copy(rel).start()

    tail = cbuf[jnp.where(high, 2 * REACH, 0), pl.ds(part, part), :]

    def gather_rows(q):
        here = quarter(q)
        products = acc[here, :] + jnp.dot(elast[here, :], tail, preferred_element_type=jnp.float32)
        return products, jnp.sum(rows_acc[here, :], axis=1, keepdims=True)

    def as_row(r):
        return jnp.transpose(jnp.broadcast_to(r, (part, 128)))[0:8, :]

    def sib_copy(which):
        q = (diag, sib)[which]
        return remote(acc.at[quarter(q)], got.at[which], fin_send.at[which], fin_recv.at[which], dev(b, sib))

    sib_row_copy = remote(r_out.at[0], r_in.at[0], fin_send.at[2], fin_recv.at[2], dev(b, sib))
    z_row_copy = remote(r_out.at[1], r_in.at[1], fin_send.at[3], fin_recv.at[3], dev(b, zp))
    z_copy = remote(z_out, z_in, fin_send.at[4], fin_recv.at[4], dev(b, zp))

    products, r = gather_rows(diag)
    acc[quarter(diag), :] = products + r * centre
    r_out[0] = as_row(r)
    sib_row_copy.start()
    sib_copy(0).start()
    products, r = gather_rows(zp)
    acc[quarter(zp), :] = products + r * centre
    r_out[1] = as_row(r)
    products, r = gather_rows(sib)
    acc[quarter(sib), :] = products + r * bb[quarter(sib), :].astype(jnp.float32)
    sib_copy(1).start()
    sib_row_copy.wait_recv()
    r_out[1] += r_in[0]
    z_row_copy.start()
    sib_copy(0).wait_recv()
    z_out[...] = (acc[quarter(zp), :] + got[0]).astype(jnp.bfloat16)
    z_copy.start()
    mine = bb[quarter(p), :].astype(jnp.float32)
    products, r = gather_rows(p)
    grad = products + r * mine
    for rel in range(3):
        loss_copy(rel).wait_recv()
    total = loss_acc[p] + loss_in[0] + loss_in[1] + loss_in[2]
    loss_out[...] = jnp.sum(jnp.sum(total, axis=1, keepdims=True), axis=0, keepdims=True) * (1.0 / count)
    sib_copy(1).wait_recv()
    z_row_copy.wait_recv()
    far = jnp.transpose(jnp.broadcast_to(r_in[1, 0:1, :], (128, part)))[:, 0:1]
    grad = grad + got[1] + far * (mine - centre)
    grad_out[...] = grad
    z_copy.wait_recv()
    far_out[...] = z_in[...]

    for chunk in range(CHUNKS):
        for way in (0, 1):
            for step in range(1, REACH + 1):
                if step == REACH and chunk in SIDE:
                    @pl.when(jnp.logical_not(is_top if way == 0 else is_bottom))
                    def _():
                        dp_copy(way, step, chunk).wait_send()
                else:
                    dp_copy(way, step, chunk).wait_send()
    for way in (0, 1):
        @pl.when(is_top if way == 0 else is_bottom)
        def _():
            for step in range(1, REACH + 1):
                for chunk in RELAYED if step < REACH else relayed_last:
                    pass_copy(way, step, chunk).wait_send()

        @pl.when(near_top if way == 0 else near_bottom)
        def _():
            for chunk in SIDE:
                side_copy(way, chunk).wait_send()
                side_pass_copy(way, chunk).wait_send()
    for chunk in (0, 1):
        for rel in range(3):
            pair_copy(rel, chunk).wait_send()
    for rel in range(3):
        loss_copy(rel).wait_send()
    sib_copy(0).wait_send()
    sib_copy(1).wait_send()
    sib_row_copy.wait_send()
    z_row_copy.wait_send()
    z_copy.wait_send()


def local_part(student, teacher, band_codes):
    part, width = student.shape
    count = 4 * part
    slots = 2 * REACH + 1
    piece = 2 * part // CHUNKS
    relayed = len(RELAYED)
    vmem = pl.BlockSpec(memory_space=pltpu.VMEM)
    anywhere = pl.BlockSpec(memory_space=pl.ANY)
    dma = pltpu.SemaphoreType.DMA
    loss, near, far = pl.pallas_call(
        kernel,
        out_shape=(
            jax.ShapeDtypeStruct((1, 1), jnp.float32),
            jax.ShapeDtypeStruct((part, width), jnp.float32),
            jax.ShapeDtypeStruct((part, width), jnp.bfloat16),
        ),
        in_specs=[anywhere, anywhere, pl.BlockSpec(memory_space=pltpu.SMEM)],
        out_specs=(vmem, vmem, vmem),
        scratch_shapes=[
            pltpu.VMEM((2 * count, width), jnp.bfloat16),
            pltpu.VMEM((slots, 2 * part, width), jnp.bfloat16),
            pltpu.VMEM((REACH, relayed, piece, width), jnp.bfloat16),
            pltpu.VMEM((len(SIDE), piece, width), jnp.bfloat16),
            pltpu.VMEM((2 * count, 128), jnp.float32),
            pltpu.VMEM((slots, 8, 2 * part), jnp.float32),
            pltpu.VMEM((2 * count, 2 * part), jnp.float32),
            pltpu.VMEM((count, 2 * part), jnp.bfloat16),
            pltpu.VMEM((count, part), jnp.bfloat16),
            pltpu.VMEM((count, width), jnp.float32),
            pltpu.VMEM((count, part), jnp.float32),
            pltpu.VMEM((REACH + 1, 8, part), jnp.float32),
            pltpu.VMEM((3, 8, part), jnp.float32),
            pltpu.VMEM((2, part, width), jnp.float32),
            pltpu.VMEM((part, width), jnp.bfloat16),
            pltpu.VMEM((part, width), jnp.bfloat16),
            pltpu.VMEM((2, 8, 128), jnp.float32),
            pltpu.VMEM((2, 8, 128), jnp.float32),
            dma((2, 2)),
            dma((2, REACH, CHUNKS)),
            dma((2, REACH, CHUNKS)),
            dma((REACH, relayed)),
            dma((REACH, relayed)),
            dma((len(SIDE),)),
            dma((len(SIDE),)),
            dma((len(SIDE),)),
            dma((3, 2)),
            dma((3, 2)),
            dma((5,)),
            dma((5,)),
            dma((3,)),
            dma((3,)),
        ],
        compiler_params=pltpu.CompilerParams(
            collective_id=0, has_side_effects=True, vmem_limit_bytes=60 * 1024 * 1024
        ),
    )(student, teacher, band_codes)
    return loss, near + far.astype(jnp.float32)


def solution(mesh):
    return jax.shard_map(
        local_part,
        mesh=mesh,
        in_specs=(P(("dp", "pair"), None), P(("dp", "pair"), None), P()),
        out_specs=(P("dp", "pair"), P(("dp", "pair"), None)),
        check_vma=False,
    )
```
